256 devices in a mesh: row: 16 (over x, y), col: 16 (over z, core).
Axes of the slice: x: 4, y: 4, z: 8, core: 2. Of those that a mesh axis runs over, the one named last changes fastest.
Arguments:
- panel_one: bfloat16 [131072, 2048], P(('row', 'col')), may hold values from -0.796875 to 0.796875
- panel_two: bfloat16 [131072, 2048], P(('row', 'col')), may hold values from -6 to 6
- inverse_one: bfloat16 [2048, 2048], P(None, 'col'), as said below
- inverse_two: bfloat16 [2048, 2048], P(None, 'col'), as said below
- update_list: int32 [256, 2], P(('row', 'col')), may hold values from -1 to 1, as said below
Outputs:
- factor_one: bfloat16 [131072, 2048], P(('row', 'col'))
- factor_two: bfloat16 [131072, 2048], P(('row', 'col'))
The draws below stay inside these ranges and needn't reach their ends.
Inputs may be any that keep to these rules, and one draw needn't show every extreme that they name: `inverse_one`: upper triangular: zero below the diagonal, diagonal entries between 0.5 and 1.5. `inverse_two`: upper triangular: zero below the diagonal, diagonal entries between 0.5 and 1.5. `update_list`: entry (d, j) names a block among the 2 first-supernode blocks of device d, or is -1 (no update). The named blocks of one device are distinct, a device's live entries come before its -1 entries, and every entry of devices 0 to 3 is live.
All inputs are finite; a program needn't handle non-finite values.
Results may differ from the reference program's by a relative error of at most 0.0056.
Values may be sent and summed in bfloat16 or wider, within the bound.
No kernel may reach another device: no remote copies, remote signals or barrier semaphores. Data moves between devices by JAX's collectives and lax.ppermute only.
A program may use at most 128 MiB of HBM per device.

```python
import jax
import jax.numpy as jnp
from jax import lax

SN = 2048
B = 256
RB1 = 2
RB2 = 2
DEVS = 256
NCB = 8


def upper_factor(key):
    key_off, key_diag = jax.random.split(key)
    off = jax.random.normal(key_off, (SN, SN), jnp.float32) * SN ** (-0.5)
    diagonal = jax.random.uniform(key_diag, (SN,), jnp.float32, 0.5, 1.5)
    return (jnp.triu(off, 1) + jnp.diag(diagonal)).astype(jnp.bfloat16)


def draw_inverse_one(key, part):
    return upper_factor(jax.random.fold_in(key, 11))


def draw_inverse_two(key, part):
    return upper_factor(jax.random.fold_in(key, 23))


def draw_update_list(key, part):
    key_order, key_count = jax.random.split(jax.random.fold_in(key, 37))
    scores = jax.random.randint(key_order, (DEVS, RB1), 0, 1 << 20) * RB1 + jnp.arange(RB1, dtype=jnp.int32)[None, :]
    order = jnp.argsort(scores, axis=1, stable=True)[:, :RB2].astype(jnp.int32)
    counts = jax.random.randint(key_count, (DEVS, 1), 1, RB2 + 1)
    device_ids = jnp.arange(DEVS, dtype=jnp.int32)[:, None]
    counts = jnp.where(device_ids < NCB // RB2, RB2, counts)
    slots = jnp.arange(RB2, dtype=jnp.int32)[None, :]
    return jnp.where(slots < counts, order, -1).astype(jnp.int32)


def level_of(own_key, extent, cuts, smallest, high):
    def one(position, blocks):
        steps = jax.random.uniform(jax.random.fold_in(jax.random.fold_in(own_key, 6), position), (blocks,), jnp.float32, smallest / len(cuts), high / len(cuts))
        return jnp.repeat(jnp.exp(steps), extent[position] // blocks).reshape((-1,) + (1,) * (len(extent) - position - 1))

    loudness = one(*cuts[0])
    for cut in cuts[1:]:
        loudness = loudness * one(*cut)
    return loudness


def noise(key, extent, spread, reach, pieces=(), kind=jnp.bfloat16):
    result = jax.random.normal(key, extent, jnp.float32) * spread
    if len(pieces) > 0:
        result = level_of(key, extent, pieces, -0.22, 0.18) * result
    return jnp.clip(result, min=-reach, max=reach).astype(kind)


def setup_inputs(seed: int = 0) -> dict:
    keys = jax.random.split(jax.random.key(seed), 6)
    panel_one = noise(keys[0], (DEVS * RB1 * B, SN), 0.13, 0.796875, ((0, 256),))
    panel_two = noise(keys[1], (DEVS * RB2 * B, SN), 1.0, 6.0, ((0, 256),))
    inverse_one = draw_inverse_one(jax.random.fold_in(keys[5], 71), 0)
    inverse_two = draw_inverse_two(jax.random.fold_in(keys[5], 71), 0)
    update_list = draw_update_list(jax.random.fold_in(keys[5], 71), 0)
    return {"panel_one": panel_one, "panel_two": panel_two, "inverse_one": inverse_one, "inverse_two": inverse_two, "update_list": update_list}


def reference(panel_one, panel_two, inverse_one, inverse_two, update_list):
    factor_one = jnp.dot(panel_one, inverse_one, preferred_element_type=jnp.float32).astype(jnp.bfloat16)
    blocks = factor_one.reshape(DEVS * RB1, B, SN)
    device_base = (jnp.arange(DEVS, dtype=jnp.int32) * RB1)[:, None]
    source = (device_base + jnp.maximum(update_list, 0)).reshape(-1).astype(jnp.int32)
    living = (update_list >= 0).reshape(-1)
    chosen = blocks[source]
    selected = jnp.where(living[:, None, None], chosen, jnp.zeros((), chosen.dtype)).reshape(DEVS * RB2 * B, SN)
    column_panel = selected[:SN]
    update = lax.dot_general(selected, column_panel, (((1,), (1,)), ((), ())), preferred_element_type=jnp.float32)
    modified = (panel_two.astype(jnp.float32) - update).astype(jnp.bfloat16)
    factor_two = jnp.dot(modified, inverse_two, preferred_element_type=jnp.float32).astype(jnp.bfloat16)
    return factor_one, factor_two
```

```python
import functools

import jax
import jax.numpy as jnp
from jax import lax
from jax.experimental import pallas as pl
from jax.experimental.pallas import tpu as pltpu
from jax.sharding import PartitionSpec as P

SN = 2048
B = 256
ROWS = 512
KEEP = 1152
PIECE = 32
BF = jnp.bfloat16
F32 = jnp.float32
AXES = ("row", "col")
SIZES = (4, 4, 8, 2)
ANY = pl.BlockSpec(memory_space=pl.ANY)
SMEM = pl.BlockSpec(memory_space=pltpu.SMEM)


def device(x, y, z, c):
    return (x * 4 + y) * 16 + z * 2 + c


def shift(dx=0, dy=0, dz=0, dc=0):
    pairs = []
    for x in range(4):
        for y in range(4):
            for z in range(8):
                for c in range(2):
                    to = device((x + dx) % 4, (y + dy) % 4, (z + dz) % 8, (c + dc) % 2)
                    pairs.append((device(x, y, z, c), to))
    return pairs


def along_z(moves):
    return [
        (r * 16 + a * 2 + c, r * 16 + b * 2 + c) for r in range(16) for a, b in moves for c in range(2)
    ]


def send(value, pairs):
    return lax.ppermute(value, AXES, pairs)


def packed(inverse):
    tail = inverse[KEEP:].reshape(7, 128, 128)[::-1].reshape(7 * 128, 128)
    pairs = [(r * 16 + c, r * 16 + 15 - c) for r in range(16) for c in range(9, 16)]
    tail = send(tail, pairs)
    return inverse[:KEEP] + jnp.concatenate([jnp.zeros((256, 128), BF), tail], axis=0)


def unpack(g, w, sems):
    for c in range(16):
        sem = sems.at[c // 2]
        count = (c | 1) + 1
        lead = min(count, 9)
        columns = pl.ds(c * 128, 128)
        pltpu.make_async_copy(
            g.at[pl.ds(c * KEEP, lead * 128)], w.at[pl.ds(0, lead * 128), columns], sem
        ).start()
        for h in range(9, count):
            pltpu.make_async_copy(
                g.at[pl.ds((15 - c) * KEEP + (17 - h) * 128, 128)],
                w.at[pl.ds(h * 128, 128), columns],
                sem,
            ).start()


def unpacked(w, sems, j):
    part = w.at[pl.ds(0, (j + 1) * 256), pl.ds(j * 256, 256)]
    pltpu.make_async_copy(part, part, sems.at[j]).wait()


def triangular_kernel(n_in, split, *refs):
    ins, g, outs = refs[:n_in], refs[n_in], refs[n_in + 1 : -6]
    x, w, o, x_sems, w_sems, o_sems = refs[-6:]
    at = 0
    copies = []
    for k, ref in enumerate(ins):
        copy = pltpu.make_async_copy(ref, x.at[pl.ds(at, ref.shape[0])], x_sems.at[k])
        copy.start()
        copies.append(copy)
        at += ref.shape[0]
    unpack(g, w, w_sems)
    for copy in copies:
        copy.wait()
    copies = []
    for j in range(8):
        unpacked(w, w_sems, j)
        columns = pl.ds(j * 256, 256)
        depth = (j + 1) * 256
        o[:, columns] = jnp.dot(
            x[:, pl.ds(0, depth)], w[pl.ds(0, depth), columns], preferred_element_type=F32
        ).astype(BF)
        for k, (ref, (start, rows)) in enumerate(zip(outs, split)):
            copy = pltpu.make_async_copy(
                o.at[pl.ds(start, rows), columns], ref.at[:, columns], o_sems.at[k, j]
            )
            copy.start()
            copies.append(copy)
    for copy in copies:
        copy.wait()


def triangular(arrays, gathered, split):
    rows = sum(a.shape[0] for a in arrays)
    return pl.pallas_call(
        functools.partial(triangular_kernel, len(arrays), split),
        out_shape=[jax.ShapeDtypeStruct((n, SN), BF) for _, n in split],
        in_specs=[ANY] * (len(arrays) + 1),
        out_specs=[ANY] * len(split),
        scratch_shapes=[
            pltpu.VMEM((rows, SN), BF),
            pltpu.VMEM((SN, SN), BF),
            pltpu.VMEM((rows, SN), BF),
            pltpu.SemaphoreType.DMA((len(arrays),)),
            pltpu.SemaphoreType.DMA((8,)),
            pltpu.SemaphoreType.DMA((len(split), 8)),
        ],
        compiler_params=pltpu.CompilerParams(vmem_limit_bytes=48 << 20),
        cost_estimate=pl.CostEstimate(
            flops=rows * SN * SN, bytes_accessed=rows * SN * 4 + (5 << 20), transcendentals=0
        ),
    )(*arrays, gathered)


PARTS = (
    (0, (0, 1, 2, 3)),
    (1, (0, 1, 2, 3)),
    (3, (0, 1, 2, 3)),
    (2, (0, 1)),
    (2, (2, 3)),
)


def final_kernel(*refs):
    place, f1, p2, g = refs[:4]
    sources = refs[4:22]
    out = refs[22]
    s, l, p, m, w, o, s_sems, l_sems, p_sem, w_sems, o_sems = refs[23:]
    x, y, core = place[0], place[1], place[2]

    first = []
    for j in range(2):
        block = jnp.maximum(place[3 + j], 0)
        copy = pltpu.make_async_copy(
            f1.at[pl.ds(pl.multiple_of(block * B, B), B)], s.at[pl.ds(j * B, B)], s_sems.at[j]
        )
        copy.start()
        first.append(copy)

    def rows_of(group):
        own, half = group // 2 == 0, group % 2
        at = (0, 1, 2, 3, 4) if half == 0 else (0, 5, 6, 7, 8)
        base = 0 if own else 9
        for k, (back, steps) in zip(at, PARTS):
            for i, step in enumerate(steps):
                row = i * PIECE + (128 if k == 0 and half else 0)
                if half == 0:
                    r = ((x + 4 - step) % 4) * 4 + (y + 4 - back) % 4
                else:
                    r = ((x + 4 - back) % 4) * 4 + (y + 4 - step) % 4
                yield sources[base + k], row, r

    def owner_of(group):
        return (core if group // 2 == 0 else 1 - core) + 2 * (group % 2)

    for group in range(4):
        base = owner_of(group) * ROWS
        for source, row, r in rows_of(group):
            pltpu.make_async_copy(
                source.at[pl.ds(row, PIECE)],
                l.at[pl.ds(pl.multiple_of(base + r * PIECE, PIECE), PIECE)],
                l_sems.at[group],
            ).start()
        if group == 0:
            p_copy = pltpu.make_async_copy(p2, p, p_sem)
            p_copy.start()
    unpack(g, w, w_sems)
    for j in range(2):
        first[j].wait()

        @pl.when(place[3 + j] < 0)
        def _(j=j):
            s[pl.ds(j * B, B), :] = jnp.zeros((B, SN), BF)

    p_copy.wait()
    for group in range(4):
        base = pl.multiple_of(owner_of(group) * ROWS, ROWS)
        part = l.at[pl.ds(base, ROWS)]
        pltpu.make_async_copy(part, part, l_sems.at[group]).wait()
        for half in range(2):
            start = pl.multiple_of(base + half * B, B)
            update = lax.dot_general(
                s[...], l[pl.ds(start, B), :], (((1,), (1,)), ((), ())), preferred_element_type=F32
            )
            columns = pl.ds(start, B)
            m[:, columns] = (p[:, columns].astype(F32) - update).astype(BF)
    copies = []
    for j in range(8):
        unpacked(w, w_sems, j)
        columns = pl.ds(j * 256, 256)
        depth = (j + 1) * 256
        o[:, columns] = jnp.dot(
            m[:, pl.ds(0, depth)], w[pl.ds(0, depth), columns], preferred_element_type=F32
        ).astype(BF)
        copy = pltpu.make_async_copy(o.at[:, columns], out.at[:, columns], o_sems.at[j])
        copy.start()
        copies.append(copy)
    for copy in copies:
        copy.wait()


def final(place, factor_one, panel_two, gathered, sources):
    square = pltpu.VMEM((SN, SN), BF)
    panel = pltpu.VMEM((ROWS, SN), BF)
    return pl.pallas_call(
        final_kernel,
        out_shape=jax.ShapeDtypeStruct((ROWS, SN), BF),
        in_specs=[SMEM] + [ANY] * (3 + len(sources)),
        out_specs=ANY,
        scratch_shapes=[
            panel,
            square,
            panel,
            panel,
            square,
            panel,
            pltpu.SemaphoreType.DMA((2,)),
            pltpu.SemaphoreType.DMA((4,)),
            pltpu.SemaphoreType.DMA,
            pltpu.SemaphoreType.DMA((8,)),
            pltpu.SemaphoreType.DMA((8,)),
        ],
        compiler_params=pltpu.CompilerParams(vmem_limit_bytes=48 << 20),
        cost_estimate=pl.CostEstimate(
            flops=3 * ROWS * SN * SN, bytes_accessed=20 << 20, transcendentals=0
        ),
    )(place, factor_one, panel_two, gathered, *sources)


def body(panel_one, panel_two, inverse_one, inverse_two, update_list):
    row, col = lax.axis_index("row"), lax.axis_index("col")
    x, y, z, core = row // 4, row % 4, col // 2, col % 2
    entries = update_list[0]

    with jax.named_scope("inverse_one"):
        full_one = lax.all_gather(packed(inverse_one), "col", axis=0, tiled=True)

    with jax.named_scope("scatter_rows"):
        pieces = []
        for r in range(16):
            start = jnp.maximum(entries[r // 8], 0) * B + (r % 8) * PIECE
            pieces.append(lax.dynamic_slice(panel_one, (start, 0), (PIECE, SN)))
        piece = jnp.where(row == 0, pieces[0], 0)
        for r in range(1, 16):
            piece = piece + send(pieces[r], [(d, r * 16 + d) for d in range(4)])

    with jax.named_scope("inverse_two"):
        full_two = lax.all_gather(packed(inverse_two), "col", axis=0, tiled=True)

    with jax.named_scope("along_z"):
        piece = jnp.where(z < 2, piece, 0)
        piece = (
            piece
            + send(piece, along_z([(0, 2), (1, 3)]))
            + send(piece, along_z([(0, 6), (1, 7)]))
            + send(piece, along_z([(0, 4), (1, 5)]))
        )
        other = send(piece, along_z([(k, k ^ 1) for k in range(8)]))
        even = z % 2 == 0
        a, b = jnp.where(even, piece, other), jnp.where(even, other, piece)

    with jax.named_scope("first_gather"):
        a_all = [a, send(a, shift(dx=1)), send(a, shift(dx=2)), send(a, shift(dx=-1))]
        b_all = [b, send(b, shift(dy=1)), send(b, shift(dy=2)), send(b, shift(dy=-1))]

    with jax.named_scope("panel_rows"):
        la, lb, lab = triangular(a_all + b_all, full_one, ((0, 128), (128, 128), (0, 256)))

    with jax.named_scope("second_gather"):
        a1, a3 = send(la, shift(dy=1)), send(la, shift(dy=-1))
        b1, b3 = send(lb, shift(dx=1)), send(lb, shift(dx=-1))
        a2t, a2b = send(a1[:64], shift(dy=1)), send(a3[64:], shift(dy=-1))
        b2t, b2b = send(b1[:64], shift(dx=1)), send(b3[64:], shift(dx=-1))
        own = [lab, a1, a3, a2t, a2b, b1, b3, b2t, b2b]
    with jax.named_scope("swap"):
        theirs = [send(v, shift(dc=1)) for v in own]

    with jax.named_scope("factor_one"):
        rows, _ = lax.optimization_barrier((panel_one, lab))
        (factor_one,) = triangular([rows], full_one, ((0, ROWS),))
    with jax.named_scope("factor_two"):
        place = jnp.stack([x, y, core, entries[0], entries[1]]).astype(jnp.int32)
        factor_two = final(place, factor_one, panel_two, full_two, own + theirs)
    return factor_one, factor_two


def solution(mesh):
    return jax.shard_map(
        body,
        mesh=mesh,
        in_specs=(
            P(("row", "col"), None),
            P(("row", "col"), None),
            P(None, "col"),
            P(None, "col"),
            P(("row", "col"), None),
        ),
        out_specs=(P(("row", "col"), None), P(("row", "col"), None)),
        check_vma=False,
    )
```

```python
import functools

import jax
import jax.numpy as jnp
from jax import lax
from jax.experimental import pallas as pl
from jax.experimental.pallas import tpu as pltpu
from jax.sharding import PartitionSpec as P

SN = 2048
B = 256
ROWS = 512
KEEP = 1152
PIECE = 32
BF = jnp.bfloat16
F32 = jnp.float32
AXES = ("row", "col")
SIZES = (4, 4, 8, 2)
ANY = pl.BlockSpec(memory_space=pl.ANY)
SMEM = pl.BlockSpec(memory_space=pltpu.SMEM)


def device(x, y, z, c):
    return (x * 4 + y) * 16 + z * 2 + c


def shift(dx=0, dy=0, dz=0, dc=0):
    pairs = []
    for x in range(4):
        for y in range(4):
            for z in range(8):
                for c in range(2):
                    to = device((x + dx) % 4, (y + dy) % 4, (z + dz) % 8, (c + dc) % 2)
                    pairs.append((device(x, y, z, c), to))
    return pairs


def along_z(moves):
    return [
        (r * 16 + a * 2 + c, r * 16 + b * 2 + c) for r in range(16) for a, b in moves for c in range(2)
    ]


def send(value, pairs):
    return lax.ppermute(value, AXES, pairs)


ORDER = (
    ((0, 0), (0, 1), (0, 2), (2, 1)),
    ((1, 0), (1, 1), (1, 3), (1, 2)),
    ((0, 3), (2, 3), (2, 2), (2, 0)),
    ((3, 0), (3, 1), (3, 3), (3, 2)),
)
NEAR = ((0, 1), (1, 0), (0, 3), (3, 0))


def in_plane(moves):
    return [(device(*a, 0, d), device(*b, 0, d)) for a, b in moves for d in range(4)]


MIRROR = [(r * 16 + c, r * 16 + 15 - c) for r in range(16) for c in range(9, 16)]


def tail_of(inverse):
    return inverse[KEEP:].reshape(7, 128, 128)[::-1].reshape(7 * 128, 128)


def packed(inverse, tail):
    return inverse[:KEEP] + jnp.concatenate([jnp.zeros((256, 128), BF), tail], axis=0)


def unpack(g, w, sems):
    for c in range(16):
        sem = sems.at[c // 2]
        count = (c | 1) + 1
        lead = min(count, 9)
        columns = pl.ds(c * 128, 128)
        pltpu.make_async_copy(
            g.at[pl.ds(c * KEEP, lead * 128)], w.at[pl.ds(0, lead * 128), columns], sem
        ).start()
        for h in range(9, count):
            pltpu.make_async_copy(
                g.at[pl.ds((15 - c) * KEEP + (17 - h) * 128, 128)],
                w.at[pl.ds(h * 128, 128), columns],
                sem,
            ).start()


def unpacked(w, sems, j):
    part = w.at[pl.ds(0, (j + 1) * 256), pl.ds(j * 256, 256)]
    pltpu.make_async_copy(part, part, sems.at[j]).wait()


def pick_kernel(place, panel, *refs):
    outs, sems = refs[:4], refs[4]
    half_b = place[5] > 0
    copies = []
    for k, group in enumerate(ORDER):
        for i, (x, y) in enumerate(group):
            rows = []
            for piece in (4 * y + x, 4 * x + y):
                rows.append(jnp.maximum(place[3 + piece // 8], 0) * B + (piece % 8) * PIECE)
            start = pl.multiple_of(jnp.where(half_b, rows[1], rows[0]), PIECE)
            copy = pltpu.make_async_copy(
                panel.at[pl.ds(start, PIECE)], outs[k].at[pl.ds(i * PIECE, PIECE)], sems.at[k, i]
            )
            copy.start()
            copies.append(copy)
    for copy in copies:
        copy.wait()


def pick(place, panel):
    return pl.pallas_call(
        pick_kernel,
        out_shape=[jax.ShapeDtypeStruct((4 * PIECE, SN), BF)] * 4,
        in_specs=[SMEM, ANY],
        out_specs=[ANY] * 4,
        scratch_shapes=[pltpu.SemaphoreType.DMA((4, 4))],
        cost_estimate=pl.CostEstimate(flops=0, bytes_accessed=4 << 20, transcendentals=0),
    )(place, panel)


def triangular_kernel(n_in, split, place, *refs):
    ins, g, outs = refs[:n_in], refs[n_in], refs[n_in + 1 : -6]
    x, w, o, x_sems, w_sems, o_sems = refs[-6:]
    copies = []
    for k, ref in enumerate(ins):
        rows = ref.shape[0]
        if n_in == 1:
            at = 0
        else:
            at = (k // 4) * 4 * rows + ((place[k // 4] + 4 - k % 4) % 4) * rows
            at = pl.multiple_of(at, rows)
        copy = pltpu.make_async_copy(ref, x.at[pl.ds(at, rows)], x_sems.at[k])
        copy.start()
        copies.append(copy)
    unpack(g, w, w_sems)
    for copy in copies:
        copy.wait()
    for j in range(8):
        unpacked(w, w_sems, j)
    copies = []
    for j in range(8):
        columns = pl.ds(j * 256, 256)
        depth = (j + 1) * 256
        o[:, columns] = jnp.dot(
            x[:, pl.ds(0, depth)], w[pl.ds(0, depth), columns], preferred_element_type=F32
        ).astype(BF)
        for k, (ref, (start, rows)) in enumerate(zip(outs, split)):
            copy = pltpu.make_async_copy(
                o.at[pl.ds(start, rows), columns], ref.at[:, columns], o_sems.at[k, j]
            )
            copy.start()
            copies.append(copy)
    for copy in copies:
        copy.wait()


def triangular(place, arrays, gathered, split, limit):
    rows = sum(a.shape[0] for a in arrays)
    return pl.pallas_call(
        functools.partial(triangular_kernel, len(arrays), split),
        out_shape=[jax.ShapeDtypeStruct((n, SN), BF) for _, n in split],
        in_specs=[SMEM] + [ANY] * (len(arrays) + 1),
        out_specs=[ANY] * len(split),
        scratch_shapes=[
            pltpu.VMEM((rows, SN), BF),
            pltpu.VMEM((SN, SN), BF),
            pltpu.VMEM((rows, SN), BF),
            pltpu.SemaphoreType.DMA((len(arrays),)),
            pltpu.SemaphoreType.DMA((8,)),
            pltpu.SemaphoreType.DMA((len(split), 8)),
        ],
        compiler_params=pltpu.CompilerParams(vmem_limit_bytes=limit << 20),
        cost_estimate=pl.CostEstimate(
            flops=rows * SN * SN, bytes_accessed=rows * SN * 4 + (5 << 20), transcendentals=0
        ),
    )(place, *arrays, gathered)


def column_of(place, own, half, back):
    core = place[2] if own else 1 - place[2]
    coordinate = place[0] if half else place[1]
    return pl.multiple_of(((2 * half + core) * 4 + (coordinate + 4 - back) % 4) * 128, 128)


FIRST = (
    ((1, 0, 0), (1, 1, 0)),
    ((0, 0, 0), (0, 1, 0)),
    ((1, 0, 1),),
    ((1, 0, 3),),
    ((1, 1, 1),),
    ((1, 1, 3),),
)
SECOND = (
    ((0, 0, 1), (0, 0, 3), (0, 1, 1), (0, 1, 3)),
    ((1, 0, 2), (1, 1, 2)),
    ((0, 0, 2), (0, 1, 2)),
)


def update_kernel(parts, last, place, f1, panel, *refs):
    g = refs[0] if last else None
    refs = refs[last:]
    sources, out = refs[: len(parts)], refs[len(parts)]
    s, l, m, w, s_sems, l_sems, m_sem, w_sems, o_sems = refs[len(parts) + 1 :]

    copies = []
    for j in range(2):
        block = jnp.maximum(place[3 + j], 0)
        copy = pltpu.make_async_copy(
            f1.at[pl.ds(pl.multiple_of(block * B, B), B)], s.at[pl.ds(j * B, B)], s_sems.at[j]
        )
        copy.start()
        copies.append(copy)
    copies.append(pltpu.make_async_copy(panel, m, m_sem))
    copies[-1].start()
    columns = []
    for k, (source, blocks) in enumerate(zip(sources, parts)):
        copy = pltpu.make_async_copy(
            source, l.at[pl.ds(len(columns) * 128, len(blocks) * 128)], l_sems.at[k]
        )
        columns += blocks
        copy.start()
        copies.append(copy)
    if last:
        unpack(g, w, w_sems)
    for copy in copies:
        copy.wait()
    for j in range(2):

        @pl.when(place[3 + j] < 0)
        def _(j=j):
            s[pl.ds(j * B, B), :] = jnp.zeros((B, SN), BF)

    for k in range(0, len(columns), 2):
        update = lax.dot_general(
            s[...], l[pl.ds(k * 128, 256), :], (((1,), (1,)), ((), ())), preferred_element_type=F32
        )
        for i in range(2):
            own = pl.ds(column_of(place, *columns[k + i]), 128)
            m[:, own] = (m[:, own].astype(F32) - update[:, i * 128 : (i + 1) * 128]).astype(BF)
    if not last:
        copy = pltpu.make_async_copy(m, out, o_sems.at[0])
        copy.start()
        copy.wait()
        return
    for j in range(8):
        unpacked(w, w_sems, j)
    copies = []
    for j in range(8):
        own = pl.ds(j * 256, 256)
        depth = (j + 1) * 256
        s[:, own] = jnp.dot(
            m[:, pl.ds(0, depth)], w[pl.ds(0, depth), own], preferred_element_type=F32
        ).astype(BF)
        copy = pltpu.make_async_copy(s.at[:, own], out.at[:, own], o_sems.at[j])
        copy.start()
        copies.append(copy)
    for copy in copies:
        copy.wait()


def updated(parts, place, factor_one, panel, gathered, sources, limit):
    last = gathered is not None
    extra = [gathered] if last else []
    rows = 128 * sum(len(blocks) for blocks in parts)
    return pl.pallas_call(
        functools.partial(update_kernel, parts, last),
        out_shape=jax.ShapeDtypeStruct((ROWS, SN), BF),
        in_specs=[SMEM] + [ANY] * (2 + len(extra) + len(sources)),
        out_specs=ANY,
        scratch_shapes=[
            pltpu.VMEM((ROWS, SN), BF),
            pltpu.VMEM((rows, SN), BF),
            pltpu.VMEM((ROWS, SN), BF),
            pltpu.VMEM((SN, SN) if last else (16, 128), BF),
            pltpu.SemaphoreType.DMA((2,)),
            pltpu.SemaphoreType.DMA((len(sources),)),
            pltpu.SemaphoreType.DMA,
            pltpu.SemaphoreType.DMA((8,)),
            pltpu.SemaphoreType.DMA((8,)),
        ],
        compiler_params=pltpu.CompilerParams(vmem_limit_bytes=limit << 20),
        cost_estimate=pl.CostEstimate(
            flops=(1 + last) * ROWS * SN * SN, bytes_accessed=(10 + 5 * last) << 20, transcendentals=0
        ),
    )(place, factor_one, panel, *extra, *sources)


def body(panel_one, panel_two, inverse_one, inverse_two, update_list):
    row, col = lax.axis_index("row"), lax.axis_index("col")
    x, y, z, core = row // 4, row % 4, col // 2, col % 2
    entries = update_list[0]
    place = jnp.stack([x, y, core, entries[0], entries[1], col // 2]).astype(jnp.int32)

    with jax.named_scope("scatter_rows"):
        groups = pick(place, panel_one)
        parts = [send(groups[k], in_plane([((0, 0), NEAR[k])])) for k in range(4)]

    with jax.named_scope("inverses"):
        tail_one = send(tail_of(inverse_one), MIRROR)
        inverse_two, tail_one = lax.optimization_barrier((inverse_two, tail_one))
        tail_two = send(tail_of(inverse_two), MIRROR)
        tail_one, *parts = lax.optimization_barrier((tail_one, *parts))
        full_one = lax.all_gather(packed(inverse_one, tail_one), "col", axis=0, tiled=True)

    with jax.named_scope("forward_rows"):
        near = parts[0] + parts[1] + parts[2] + parts[3]
        kept = jnp.where(row == NEAR[0][1], near[32:64], near[:32])
        piece = jnp.where(row == 0, groups[0][:32], kept)
        for i in range(1, 4):
            moves = [(NEAR[k], ORDER[k][i]) for k in range(4) if NEAR[k] != ORDER[k][i]]
            piece = piece + send(near[i * 32 : (i + 1) * 32], in_plane(moves))

    with jax.named_scope("inverses"):
        tail_two, piece = lax.optimization_barrier((tail_two, piece))
        full_two = lax.all_gather(packed(inverse_two, tail_two), "col", axis=0, tiled=True)

    with jax.named_scope("along_z"):
        piece = jnp.where(z < 2, piece, 0)
        piece = (
            piece
            + send(piece, along_z([(0, 2), (1, 3)]))
            + send(piece, along_z([(0, 6), (1, 7)]))
            + send(piece, along_z([(0, 4), (1, 5)]))
        )
        other = send(piece, along_z([(k, k ^ 1) for k in range(8)]))
        even = z % 2 == 0
        a, b = jnp.where(even, piece, other), jnp.where(even, other, piece)

    with jax.named_scope("first_gather"):
        a_all = [a, send(a, shift(dx=1)), send(a, shift(dx=2)), send(a, shift(dx=-1))]
        b_all = [b, send(b, shift(dy=1)), send(b, shift(dy=2)), send(b, shift(dy=-1))]

    with jax.named_scope("panel_rows"):
        split = ((0, 128), (128, 128), (0, 256))
        la, lb, lab = triangular(place, a_all + b_all, full_one, split, 58)

    with jax.named_scope("factor_one"):
        rows, _ = lax.optimization_barrier((panel_one, lab))
        (factor_one,) = triangular(place, [rows], full_one, ((0, ROWS),), 40)

    with jax.named_scope("second_gather"):
        a1, a3 = send(la, shift(dy=1)), send(la, shift(dy=-1))
        b1, b3 = send(lb, shift(dx=1)), send(lb, shift(dx=-1))
        theirs = send(lab, shift(dc=1))
        a1, a3, b1, b3, factor_one = lax.optimization_barrier((a1, a3, b1, b3, factor_one))
        halves = [
            send(a1[:64], shift(dy=1)),
            send(a3[64:], shift(dy=-1)),
            send(b1[:64], shift(dx=1)),
            send(b3[64:], shift(dx=-1)),
        ]
        swapped = send(jnp.concatenate([a1, a3, b1, b3]), shift(dc=1))
    with jax.named_scope("update"):
        first = [lab, theirs, a1, a3, b1, b3]
        modified = updated(FIRST, place, factor_one, panel_two, None, first, 40)
    with jax.named_scope("swap"):
        *halves, modified = lax.optimization_barrier((*halves, modified))
        halves = jnp.concatenate(halves)
        swapped_halves = send(halves, shift(dc=1))
    with jax.named_scope("factor_two"):
        second = [swapped, halves, swapped_halves]
        factor_two = updated(SECOND, place, factor_one, modified, full_two, second, 58)
    return factor_one, factor_two


def solution(mesh):
    return jax.shard_map(
        body,
        mesh=mesh,
        in_specs=(
            P(("row", "col"), None),
            P(("row", "col"), None),
            P(None, "col"),
            P(None, "col"),
            P(("row", "col"), None),
        ),
        out_specs=(P(("row", "col"), None), P(("row", "col"), None)),
        check_vma=False,
    )
```

```python
import functools

import jax
import jax.numpy as jnp
from jax import lax
from jax.experimental import pallas as pl
from jax.experimental.pallas import tpu as pltpu
from jax.sharding import PartitionSpec as P

SN = 2048
B = 256
ROWS = 512
KEEP = 1152
PIECE = 32
BF = jnp.bfloat16
F32 = jnp.float32
AXES = ("row", "col")
SIZES = (4, 4, 8, 2)
ANY = pl.BlockSpec(memory_space=pl.ANY)
SMEM = pl.BlockSpec(memory_space=pltpu.SMEM)


def device(x, y, z, c):
    return (x * 4 + y) * 16 + z * 2 + c


def shift(dx=0, dy=0, dz=0, dc=0):
    pairs = []
    for x in range(4):
        for y in range(4):
            for z in range(8):
                for c in range(2):
                    to = device((x + dx) % 4, (y + dy) % 4, (z + dz) % 8, (c + dc) % 2)
                    pairs.append((device(x, y, z, c), to))
    return pairs


def along_z(moves):
    return [
        (r * 16 + a * 2 + c, r * 16 + b * 2 + c) for r in range(16) for a, b in moves for c in range(2)
    ]


def send(value, pairs):
    return lax.ppermute(value, AXES, pairs)


ORDER = (
    ((0, 0), (0, 1), (0, 2), (2, 1)),
    ((1, 0), (1, 1), (1, 3), (1, 2)),
    ((0, 3), (2, 3), (2, 2), (2, 0)),
    ((3, 0), (3, 1), (3, 3), (3, 2)),
)
NEAR = ((0, 1), (1, 0), (0, 3), (3, 0))


def in_plane(moves):
    return [(device(*a, 0, d), device(*b, 0, d)) for a, b in moves for d in range(4)]


MIRROR = [(r * 16 + c, r * 16 + 15 - c) for r in range(16) for c in range(9, 16)]


def tail_of(inverse):
    return inverse[KEEP:].reshape(7, 128, 128)[::-1].reshape(7 * 128, 128)


def packed(inverse, tail):
    return inverse[:KEEP] + jnp.concatenate([jnp.zeros((256, 128), BF), tail], axis=0)


def unpack_square(g, w, sems):
    for c in range(16):
        rows = ((c | 1) + 1) * 128
        pltpu.make_async_copy(
            g.at[pl.ds(c * SN, rows)], w.at[pl.ds(0, rows), pl.ds(c * 128, 128)], sems.at[c // 2]
        ).start()


def unpack(g, w, sems):
    for c in range(16):
        sem = sems.at[c // 2]
        count = (c | 1) + 1
        lead = min(count, 9)
        columns = pl.ds(c * 128, 128)
        pltpu.make_async_copy(
            g.at[pl.ds(c * KEEP, lead * 128)], w.at[pl.ds(0, lead * 128), columns], sem
        ).start()
        for h in range(9, count):
            pltpu.make_async_copy(
                g.at[pl.ds((15 - c) * KEEP + (17 - h) * 128, 128)],
                w.at[pl.ds(h * 128, 128), columns],
                sem,
            ).start()


def unpacked(w, sems, j):
    part = w.at[pl.ds(0, (j + 1) * 256), pl.ds(j * 256, 256)]
    pltpu.make_async_copy(part, part, sems.at[j]).wait()


def position():
    row, col = lax.axis_index("row"), lax.axis_index("col")
    return row // 4, row % 4, col // 2, col % 2


def pick_kernel(entries, panel, *refs):
    outs, sems = refs[:4], refs[4]
    half_b = position()[2] > 0
    copies = []
    for k, group in enumerate(ORDER):
        for i, (x, y) in enumerate(group):
            rows = []
            for piece in (4 * y + x, 4 * x + y):
                rows.append(jnp.maximum(entries[0, piece // 8], 0) * B + (piece % 8) * PIECE)
            start = pl.multiple_of(jnp.where(half_b, rows[1], rows[0]), PIECE)
            copy = pltpu.make_async_copy(
                panel.at[pl.ds(start, PIECE)], outs[k].at[pl.ds(i * PIECE, PIECE)], sems.at[k, i]
            )
            copy.start()
            copies.append(copy)
    for copy in copies:
        copy.wait()


def pick(entries, panel):
    return pl.pallas_call(
        pick_kernel,
        out_shape=[jax.ShapeDtypeStruct((4 * PIECE, SN), BF)] * 4,
        in_specs=[SMEM, ANY],
        out_specs=[pl.BlockSpec(memory_space=pltpu.VMEM)] * 4,
        scratch_shapes=[pltpu.SemaphoreType.DMA((4, 4))],
        compiler_params=pltpu.CompilerParams(vmem_limit_bytes=8 << 20),
        cost_estimate=pl.CostEstimate(flops=0, bytes_accessed=4 << 20, transcendentals=0),
    )(entries, panel)


def triangular_kernel(n_in, split, *refs):
    place = position()[:2]
    ins, g, outs = refs[:n_in], refs[n_in], refs[n_in + 1 : -6]
    x, w, o, x_sems, w_sems, o_sems = refs[-6:]
    copies = []
    for k, ref in enumerate(ins):
        rows = ref.shape[0]
        if n_in == 1:
            at = 0
        else:
            at = (k // 4) * 4 * rows + ((place[k // 4] + 4 - k % 4) % 4) * rows
            at = pl.multiple_of(at, rows)
        copy = pltpu.make_async_copy(ref, x.at[pl.ds(at, rows)], x_sems.at[k])
        copy.start()
        copies.append(copy)
    unpack_square(g, w, w_sems)
    for copy in copies:
        copy.wait()
    for j in range(8):
        unpacked(w, w_sems, j)
    copies = []
    for j in range(8):
        columns = pl.ds(j * 256, 256)
        depth = (j + 1) * 256
        o[:, columns] = jnp.dot(
            x[:, pl.ds(0, depth)], w[pl.ds(0, depth), columns], preferred_element_type=F32
        ).astype(BF)
        for k, (ref, (start, rows)) in enumerate(zip(outs, split)):
            copy = pltpu.make_async_copy(
                o.at[pl.ds(start, rows), columns], ref.at[:, columns], o_sems.at[k, j]
            )
            copy.start()
            copies.append(copy)
    for copy in copies:
        copy.wait()


def triangular(arrays, gathered, split, limit):
    rows = sum(a.shape[0] for a in arrays)
    return pl.pallas_call(
        functools.partial(triangular_kernel, len(arrays), split),
        out_shape=[jax.ShapeDtypeStruct((n, SN), BF) for _, n in split],
        in_specs=[ANY] * (len(arrays) + 1),
        out_specs=[ANY] * len(split),
        scratch_shapes=[
            pltpu.VMEM((rows, SN), BF),
            pltpu.VMEM((SN, SN), BF),
            pltpu.VMEM((rows, SN), BF),
            pltpu.SemaphoreType.DMA((len(arrays),)),
            pltpu.SemaphoreType.DMA((8,)),
            pltpu.SemaphoreType.DMA((len(split), 8)),
        ],
        compiler_params=pltpu.CompilerParams(vmem_limit_bytes=limit << 20),
        cost_estimate=pl.CostEstimate(
            flops=rows * SN * SN, bytes_accessed=rows * SN * 4 + (5 << 20), transcendentals=0
        ),
    )(*arrays, gathered)


def column_of(place, own, half, back):
    core = place[3] if own else 1 - place[3]
    coordinate = place[0] if half else place[1]
    return pl.multiple_of(((2 * half + core) * 4 + (coordinate + 4 - back) % 4) * 128, 128)


FIRST = (
    ((1, 0, 0), (1, 1, 0)),
    ((0, 0, 0), (0, 1, 0)),
    ((1, 0, 1),),
    ((1, 0, 3),),
    ((1, 1, 1),),
    ((1, 1, 3),),
)
SECOND = (
    ((0, 0, 1), (0, 0, 3), (0, 1, 1), (0, 1, 3)),
    ((1, 0, 2), (1, 1, 2)),
    ((0, 0, 2), (0, 1, 2)),
)


def update_kernel(parts, last, entries, f1, panel, *refs):
    place = position()
    g = refs[0] if last else None
    refs = refs[last:]
    sources, out = refs[: len(parts)], refs[len(parts)]
    s, l, m, w, s_sems, l_sems, m_sem, w_sems, o_sems = refs[len(parts) + 1 :]

    copies = []
    for j in range(2):
        block = jnp.maximum(entries[0, j], 0)
        copy = pltpu.make_async_copy(
            f1.at[pl.ds(pl.multiple_of(block * B, B), B)], s.at[pl.ds(j * B, B)], s_sems.at[j]
        )
        copy.start()
        copies.append(copy)
    columns = []
    for k, (source, blocks) in enumerate(zip(sources, parts)):
        copy = pltpu.make_async_copy(
            source, l.at[pl.ds(len(columns) * 128, len(blocks) * 128)], l_sems.at[k]
        )
        columns += blocks
        copy.start()
        copies.append(copy)
    copies.append(pltpu.make_async_copy(panel, m, m_sem))
    copies[-1].start()
    for copy in copies:
        copy.wait()
    if last:
        unpack(g, w, w_sems)
    for j in range(2):

        @pl.when(entries[0, j] < 0)
        def _(j=j):
            s[pl.ds(j * B, B), :] = jnp.zeros((B, SN), BF)

    for k in range(0, len(columns), 2):
        update = lax.dot_general(
            s[...], l[pl.ds(k * 128, 256), :], (((1,), (1,)), ((), ())), preferred_element_type=F32
        )
        for i in range(2):
            own = pl.ds(column_of(place, *columns[k + i]), 128)
            m[:, own] = (m[:, own].astype(F32) - update[:, i * 128 : (i + 1) * 128]).astype(BF)
    if not last:
        copy = pltpu.make_async_copy(m, out, o_sems.at[0])
        copy.start()
        copy.wait()
        return
    for j in range(8):
        unpacked(w, w_sems, j)
    copies = []
    for j in range(8):
        own = pl.ds(j * 256, 256)
        depth = (j + 1) * 256
        s[:, own] = jnp.dot(
            m[:, pl.ds(0, depth)], w[pl.ds(0, depth), own], preferred_element_type=F32
        ).astype(BF)
        copy = pltpu.make_async_copy(s.at[:, own], out.at[:, own], o_sems.at[j])
        copy.start()
        copies.append(copy)
    for copy in copies:
        copy.wait()


def updated(parts, entries, factor_one, panel, gathered, sources, limit):
    last = gathered is not None
    extra = [gathered] if last else []
    rows = 128 * sum(len(blocks) for blocks in parts)
    return pl.pallas_call(
        functools.partial(update_kernel, parts, last),
        out_shape=jax.ShapeDtypeStruct((ROWS, SN), BF),
        in_specs=[SMEM] + [ANY] * (2 + len(extra) + len(sources)),
        out_specs=ANY,
        scratch_shapes=[
            pltpu.VMEM((ROWS, SN), BF),
            pltpu.VMEM((rows, SN), BF),
            pltpu.VMEM((ROWS, SN), BF),
            pltpu.VMEM((SN, SN) if last else (16, 128), BF),
            pltpu.SemaphoreType.DMA((2,)),
            pltpu.SemaphoreType.DMA((len(sources),)),
            pltpu.SemaphoreType.DMA,
            pltpu.SemaphoreType.DMA((8,)),
            pltpu.SemaphoreType.DMA((8,)),
        ],
        compiler_params=pltpu.CompilerParams(vmem_limit_bytes=limit << 20),
        cost_estimate=pl.CostEstimate(
            flops=(1 + last) * ROWS * SN * SN, bytes_accessed=(10 + 5 * last) << 20, transcendentals=0
        ),
    )(entries, factor_one, panel, *extra, *sources)


def body(panel_one, panel_two, inverse_one, inverse_two, update_list):
    row, col = lax.axis_index("row"), lax.axis_index("col")
    z = col // 2

    with jax.named_scope("inverse_one"):
        full_one = lax.all_gather(inverse_one, "col", axis=0, tiled=True)

    with jax.named_scope("scatter_rows"):
        groups = pick(update_list, panel_one)
        parts = [send(groups[k], in_plane([((0, 0), NEAR[k])])) for k in range(4)]

    with jax.named_scope("inverse_two"):
        tail = send(tail_of(inverse_two), MIRROR)
        tail, *parts = lax.optimization_barrier((tail, *parts))

    with jax.named_scope("forward_rows"):
        near = parts[0] + parts[1] + parts[2] + parts[3]
        kept = jnp.where(row == NEAR[0][1], near[32:64], near[:32])
        piece = jnp.where(row == 0, groups[0][:32], kept)
        for i in range(1, 4):
            moves = [(NEAR[k], ORDER[k][i]) for k in range(4) if NEAR[k] != ORDER[k][i]]
            piece = piece + send(near[i * 32 : (i + 1) * 32], in_plane(moves))

    with jax.named_scope("inverse_two"):
        full_two = lax.all_gather(packed(inverse_two, tail), "col", axis=0, tiled=True)

    with jax.named_scope("along_z"):
        piece = jnp.where(z < 2, piece, 0)
        piece = (
            piece
            + send(piece, along_z([(0, 2), (1, 3)]))
            + send(piece, along_z([(0, 6), (1, 7)]))
            + send(piece, along_z([(0, 4), (1, 5)]))
        )
        other = send(piece, along_z([(k, k ^ 1) for k in range(8)]))
        even = z % 2 == 0
        a, b = jnp.where(even, piece, other), jnp.where(even, other, piece)

    with jax.named_scope("first_gather"):
        a_all = [a, send(a, shift(dx=1)), send(a, shift(dx=2)), send(a, shift(dx=-1))]
        b_all = [b, send(b, shift(dy=1)), send(b, shift(dy=2)), send(b, shift(dy=-1))]

    with jax.named_scope("panel_rows"):
        split = ((0, 128), (128, 128), (0, 256))
        la, lb, lab = triangular(a_all + b_all, full_one, split, 58)

    with jax.named_scope("factor_one"):
        rows, _ = lax.optimization_barrier((panel_one, lab))
        (factor_one,) = triangular([rows], full_one, ((0, ROWS),), 40)

    with jax.named_scope("second_gather"):
        a1, a3 = send(la, shift(dy=1)), send(la, shift(dy=-1))
        b1, b3 = send(lb, shift(dx=1)), send(lb, shift(dx=-1))
        theirs = send(lab, shift(dc=1))
        a1, a3, b1, b3, factor_one = lax.optimization_barrier((a1, a3, b1, b3, factor_one))
        halves = [
            send(a1[:64], shift(dy=1)),
            send(a3[64:], shift(dy=-1)),
            send(b1[:64], shift(dx=1)),
            send(b3[64:], shift(dx=-1)),
        ]
        swapped = send(jnp.concatenate([a1, a3, b1, b3]), shift(dc=1))
    with jax.named_scope("update"):
        first = [lab, theirs, a1, a3, b1, b3]
        modified = updated(FIRST, update_list, factor_one, panel_two, None, first, 40)
    with jax.named_scope("swap"):
        *halves, modified = lax.optimization_barrier((*halves, modified))
        halves = jnp.concatenate(halves)
        swapped_halves = send(halves, shift(dc=1))
    with jax.named_scope("factor_two"):
        second = [swapped, halves, swapped_halves]
        factor_two = updated(SECOND, update_list, factor_one, modified, full_two, second, 58)
    return factor_one, factor_two


def solution(mesh):
    return jax.shard_map(
        body,
        mesh=mesh,
        in_specs=(
            P(("row", "col"), None),
            P(("row", "col"), None),
            P(None, "col"),
            P(None, "col"),
            P(("row", "col"), None),
        ),
        out_specs=(P(("row", "col"), None), P(("row", "col"), None)),
        check_vma=False,
    )
```

```python
import functools

import jax
import jax.numpy as jnp
from jax import lax
from jax.experimental import pallas as pl
from jax.experimental.pallas import tpu as pltpu
from jax.sharding import PartitionSpec as P

SN = 2048
B = 256
ROWS = 512
KEEP = 1152
PIECE = 32
BF = jnp.bfloat16
F32 = jnp.float32
AXES = ("row", "col")
SIZES = (4, 4, 8, 2)
ANY = pl.BlockSpec(memory_space=pl.ANY)
SMEM = pl.BlockSpec(memory_space=pltpu.SMEM)


def device(x, y, z, c):
    return (x * 4 + y) * 16 + z * 2 + c


def shift(dx=0, dy=0, dz=0, dc=0):
    pairs = []
    for x in range(4):
        for y in range(4):
            for z in range(8):
                for c in range(2):
                    to = device((x + dx) % 4, (y + dy) % 4, (z + dz) % 8, (c + dc) % 2)
                    pairs.append((device(x, y, z, c), to))
    return pairs


def along_z(moves):
    return [
        (r * 16 + a * 2 + c, r * 16 + b * 2 + c) for r in range(16) for a, b in moves for c in range(2)
    ]


def send(value, pairs):
    return lax.ppermute(value, AXES, pairs)


ORDER = (
    ((0, 0), (0, 1), (0, 2), (2, 1)),
    ((1, 0), (1, 1), (1, 3), (1, 2)),
    ((0, 3), (2, 3), (2, 2), (2, 0)),
    ((3, 0), (3, 1), (3, 3), (3, 2)),
)
NEAR = ((0, 1), (1, 0), (0, 3), (3, 0))


def in_plane(moves):
    return [(device(*a, 0, d), device(*b, 0, d)) for a, b in moves for d in range(4)]


MIRROR = [(r * 16 + c, r * 16 + 15 - c) for r in range(16) for c in range(9, 16)]


def tail_of(inverse):
    return inverse[KEEP:].reshape(7, 128, 128)[::-1].reshape(7 * 128, 128)


def packed(inverse, tail):
    return inverse[:KEEP] + jnp.concatenate([jnp.zeros((256, 128), BF), tail], axis=0)


def unpack_square(g, w, sems):
    for c in range(16):
        rows = ((c | 1) + 1) * 128
        pltpu.make_async_copy(
            g.at[pl.ds(c * SN, rows)], w.at[pl.ds(0, rows), pl.ds(c * 128, 128)], sems.at[c // 2]
        ).start()


def unpack(g, w, sems):
    for c in range(16):
        sem = sems.at[c // 2]
        count = (c | 1) + 1
        lead = min(count, 9)
        columns = pl.ds(c * 128, 128)
        pltpu.make_async_copy(
            g.at[pl.ds(c * KEEP, lead * 128)], w.at[pl.ds(0, lead * 128), columns], sem
        ).start()
        for h in range(9, count):
            pltpu.make_async_copy(
                g.at[pl.ds((15 - c) * KEEP + (17 - h) * 128, 128)],
                w.at[pl.ds(h * 128, 128), columns],
                sem,
            ).start()


def unpacked(w, sems, j):
    part = w.at[pl.ds(0, (j + 1) * 256), pl.ds(j * 256, 256)]
    pltpu.make_async_copy(part, part, sems.at[j]).wait()


def position():
    row, col = lax.axis_index("row"), lax.axis_index("col")
    return row // 4, row % 4, col // 2, col % 2


def pick_kernel(entries, panel, *refs):
    outs = refs[:4]
    rows, in_sems, sems = refs[4:]
    half_b = position()[2] > 0
    copies = []
    for j in range(2):
        start = pl.multiple_of(jnp.maximum(entries[0, j], 0) * B, B)
        copy = pltpu.make_async_copy(
            panel.at[pl.ds(start, B)], rows.at[pl.ds(j * B, B)], in_sems.at[j]
        )
        copy.start()
        copies.append(copy)
    for copy in copies:
        copy.wait()
    copies = []
    for k, group in enumerate(ORDER):
        for i, (x, y) in enumerate(group):
            start = jnp.where(half_b, 4 * x + y, 4 * y + x) * PIECE
            copy = pltpu.make_async_copy(
                rows.at[pl.ds(pl.multiple_of(start, PIECE), PIECE)],
                outs[k].at[pl.ds(i * PIECE, PIECE)],
                sems.at[k, i],
            )
            copy.start()
            copies.append(copy)
    for copy in copies:
        copy.wait()


def pick(entries, panel):
    return pl.pallas_call(
        pick_kernel,
        out_shape=[jax.ShapeDtypeStruct((4 * PIECE, SN), BF)] * 4,
        in_specs=[SMEM, ANY],
        out_specs=[ANY] * 4,
        scratch_shapes=[
            pltpu.VMEM((ROWS, SN), BF),
            pltpu.SemaphoreType.DMA((2,)),
            pltpu.SemaphoreType.DMA((4, 4)),
        ],
        compiler_params=pltpu.CompilerParams(vmem_limit_bytes=40 << 20),
        cost_estimate=pl.CostEstimate(flops=0, bytes_accessed=4 << 20, transcendentals=0),
    )(entries, panel)


def halves_kernel(*refs):
    ins, outs = refs[:4], refs[4:8]
    whole, rows, in_sems, sems, whole_sem = refs[8:]
    copies = []
    for k in range(4):
        copy = pltpu.make_async_copy(ins[k], rows.at[pl.ds(k * 128, 128)], in_sems.at[k])
        copy.start()
        copies.append(copy)
    for k in range(4):
        copies[k].wait()
        copy = pltpu.make_async_copy(
            rows.at[pl.ds(k * 128 + k % 2 * 64, 64)], outs[k], sems.at[k]
        )
        copy.start()
        copies.append(copy)
    copy = pltpu.make_async_copy(rows, whole, whole_sem)
    copy.start()
    copies.append(copy)
    for copy in copies[4:]:
        copy.wait()


def halves_of(arrays):
    return pl.pallas_call(
        halves_kernel,
        out_shape=[jax.ShapeDtypeStruct((64, SN), BF)] * 4 + [jax.ShapeDtypeStruct((512, SN), BF)],
        in_specs=[ANY] * 4,
        out_specs=[ANY] * 5,
        scratch_shapes=[
            pltpu.VMEM((512, SN), BF),
            pltpu.SemaphoreType.DMA((4,)),
            pltpu.SemaphoreType.DMA((4,)),
            pltpu.SemaphoreType.DMA,
        ],
        compiler_params=pltpu.CompilerParams(vmem_limit_bytes=8 << 20),
        cost_estimate=pl.CostEstimate(flops=0, bytes_accessed=5 << 20, transcendentals=0),
    )(*arrays)


def triangular_kernel(n_in, split, *refs):
    place = position()[:2]
    ins, g, outs = refs[:n_in], refs[n_in], refs[n_in + 1 : -6]
    x, w, o, x_sems, w_sems, o_sems = refs[-6:]
    copies = []
    for k, ref in enumerate(ins):
        rows = ref.shape[0]
        if n_in == 1:
            at = 0
        else:
            at = (k // 4) * 4 * rows + ((place[k // 4] + 4 - k % 4) % 4) * rows
            at = pl.multiple_of(at, rows)
        copy = pltpu.make_async_copy(ref, x.at[pl.ds(at, rows)], x_sems.at[k])
        copy.start()
        copies.append(copy)
    unpack_square(g, w, w_sems)
    for copy in copies:
        copy.wait()
    for j in range(8):
        unpacked(w, w_sems, j)
    copies = []
    for j in range(8):
        columns = pl.ds(j * 256, 256)
        depth = (j + 1) * 256
        o[:, columns] = jnp.dot(
            x[:, pl.ds(0, depth)], w[pl.ds(0, depth), columns], preferred_element_type=F32
        ).astype(BF)
        for k, (ref, (start, rows)) in enumerate(zip(outs, split)):
            copy = pltpu.make_async_copy(
                o.at[pl.ds(start, rows), columns], ref.at[:, columns], o_sems.at[k, j]
            )
            copy.start()
            copies.append(copy)
    for copy in copies:
        copy.wait()


def triangular(arrays, gathered, split, limit):
    rows = sum(a.shape[0] for a in arrays)
    return pl.pallas_call(
        functools.partial(triangular_kernel, len(arrays), split),
        out_shape=[jax.ShapeDtypeStruct((n, SN), BF) for _, n in split],
        in_specs=[ANY] * (len(arrays) + 1),
        out_specs=[ANY] * len(split),
        scratch_shapes=[
            pltpu.VMEM((rows, SN), BF),
            pltpu.VMEM((SN, SN), BF),
            pltpu.VMEM((rows, SN), BF),
            pltpu.SemaphoreType.DMA((len(arrays),)),
            pltpu.SemaphoreType.DMA((8,)),
            pltpu.SemaphoreType.DMA((len(split), 8)),
        ],
        compiler_params=pltpu.CompilerParams(vmem_limit_bytes=limit << 20),
        cost_estimate=pl.CostEstimate(
            flops=rows * SN * SN, bytes_accessed=rows * SN * 4 + (5 << 20), transcendentals=0
        ),
    )(*arrays, gathered)


def column_of(place, own, half, back):
    core = place[3] if own else 1 - place[3]
    coordinate = place[0] if half else place[1]
    return pl.multiple_of(((2 * half + core) * 4 + (coordinate + 4 - back) % 4) * 128, 128)


FIRST = (
    ((1, 0, 0), (1, 1, 0)),
    ((0, 0, 0), (0, 1, 0)),
    ((1, 0, 1),),
    ((1, 0, 3),),
    ((1, 1, 1),),
    ((1, 1, 3),),
)
SECOND = (
    ((0, 0, 1), (0, 0, 3), (0, 1, 1), (0, 1, 3)),
    ((1, 0, 2), (1, 1, 2)),
    ((0, 0, 2), (0, 1, 2)),
)


def update_kernel(parts, last, entries, f1, panel, *refs):
    place = position()
    g = refs[0] if last else None
    refs = refs[last:]
    sources, out = refs[: len(parts)], refs[len(parts)]
    s, l, m, w, s_sems, l_sems, m_sem, w_sems, o_sems = refs[len(parts) + 1 :]

    copies = []
    for j in range(2):
        block = jnp.maximum(entries[0, j], 0)
        copy = pltpu.make_async_copy(
            f1.at[pl.ds(pl.multiple_of(block * B, B), B)], s.at[pl.ds(j * B, B)], s_sems.at[j]
        )
        copy.start()
        copies.append(copy)
    columns, first = [], {}
    for k, (source, blocks) in enumerate(zip(sources, parts)):
        copy = pltpu.make_async_copy(
            source, l.at[pl.ds(len(columns) * 128, len(blocks) * 128)], l_sems.at[k]
        )
        first[len(columns)] = copy
        columns += blocks
        copy.start()
        if k == 0:
            copies.append(pltpu.make_async_copy(panel, m, m_sem))
            copies[-1].start()
    for copy in copies:
        copy.wait()
    if last:
        unpack(g, w, w_sems)
    for j in range(2):

        @pl.when(entries[0, j] < 0)
        def _(j=j):
            s[pl.ds(j * B, B), :] = jnp.zeros((B, SN), BF)

    for k in range(0, len(columns), 2):
        for i in (k, k + 1):
            if i in first:
                first[i].wait()
        update = lax.dot_general(
            s[...], l[pl.ds(k * 128, 256), :], (((1,), (1,)), ((), ())), preferred_element_type=F32
        )
        for i in range(2):
            own = pl.ds(column_of(place, *columns[k + i]), 128)
            m[:, own] = (m[:, own].astype(F32) - update[:, i * 128 : (i + 1) * 128]).astype(BF)
    if not last:
        copy = pltpu.make_async_copy(m, out, o_sems.at[0])
        copy.start()
        copy.wait()
        return
    for j in range(8):
        unpacked(w, w_sems, j)
    copies = []
    for j in range(8):
        own = pl.ds(j * 256, 256)
        depth = (j + 1) * 256
        s[:, own] = jnp.dot(
            m[:, pl.ds(0, depth)], w[pl.ds(0, depth), own], preferred_element_type=F32
        ).astype(BF)
        copy = pltpu.make_async_copy(s.at[:, own], out.at[:, own], o_sems.at[j])
        copy.start()
        copies.append(copy)
    for copy in copies:
        copy.wait()


def updated(parts, entries, factor_one, panel, gathered, sources, limit):
    last = gathered is not None
    extra = [gathered] if last else []
    rows = 128 * sum(len(blocks) for blocks in parts)
    return pl.pallas_call(
        functools.partial(update_kernel, parts, last),
        out_shape=jax.ShapeDtypeStruct((ROWS, SN), BF),
        in_specs=[SMEM] + [ANY] * (2 + len(extra) + len(sources)),
        out_specs=ANY,
        scratch_shapes=[
            pltpu.VMEM((ROWS, SN), BF),
            pltpu.VMEM((rows, SN), BF),
            pltpu.VMEM((ROWS, SN), BF),
            pltpu.VMEM((SN, SN) if last else (16, 128), BF),
            pltpu.SemaphoreType.DMA((2,)),
            pltpu.SemaphoreType.DMA((len(sources),)),
            pltpu.SemaphoreType.DMA,
            pltpu.SemaphoreType.DMA((8,)),
            pltpu.SemaphoreType.DMA((8,)),
        ],
        compiler_params=pltpu.CompilerParams(vmem_limit_bytes=limit << 20),
        cost_estimate=pl.CostEstimate(
            flops=(1 + last) * ROWS * SN * SN, bytes_accessed=(10 + 5 * last) << 20, transcendentals=0
        ),
    )(entries, factor_one, panel, *extra, *sources)


def body(panel_one, panel_two, inverse_one, inverse_two, update_list):
    row, col = lax.axis_index("row"), lax.axis_index("col")
    z = col // 2

    with jax.named_scope("inverse_one"):
        full_one = lax.all_gather(inverse_one, "col", axis=0, tiled=True)

    with jax.named_scope("scatter_rows"):
        groups = pick(update_list, panel_one)
        parts = [send(groups[k], in_plane([((0, 0), NEAR[k])])) for k in range(4)]

    with jax.named_scope("forward_rows"):
        near = parts[0] + parts[1] + parts[2] + parts[3]
        kept = jnp.where(row == NEAR[0][1], near[32:64], near[:32])
        piece = jnp.where(row == 0, groups[0][:32], kept)
        for i in range(1, 4):
            moves = [(NEAR[k], ORDER[k][i]) for k in range(4) if NEAR[k] != ORDER[k][i]]
            piece = piece + send(near[i * 32 : (i + 1) * 32], in_plane(moves))

    with jax.named_scope("along_z"):
        piece = jnp.where(z < 2, piece, 0)
        piece = (
            piece
            + send(piece, along_z([(0, 2), (1, 3)]))
            + send(piece, along_z([(0, 6), (1, 7)]))
            + send(piece, along_z([(0, 4), (1, 5)]))
        )
        other = send(piece, along_z([(k, k ^ 1) for k in range(8)]))
        even = z % 2 == 0
        a, b = jnp.where(even, piece, other), jnp.where(even, other, piece)

    with jax.named_scope("inverse_two"):
        inverse_two, a, b = lax.optimization_barrier((inverse_two, a, b))
        tail = send(tail_of(inverse_two), MIRROR)

    with jax.named_scope("first_gather"):
        a_all = [a, send(a, shift(dx=1)), send(a, shift(dx=2)), send(a, shift(dx=-1))]
        b_all = [b, send(b, shift(dy=1)), send(b, shift(dy=2)), send(b, shift(dy=-1))]

    with jax.named_scope("inverse_two"):
        tail, *_ = lax.optimization_barrier((tail, *a_all, *b_all))
        full_two = lax.all_gather(packed(inverse_two, tail), "col", axis=0, tiled=True)

    with jax.named_scope("panel_rows"):
        split = ((0, 128), (128, 128), (0, 256))
        la, lb, lab = triangular(a_all + b_all, full_one, split, 58)

    with jax.named_scope("factor_one"):
        rows, _ = lax.optimization_barrier((panel_one, lab))
        (factor_one,) = triangular([rows], full_one, ((0, ROWS),), 58)

    with jax.named_scope("second_gather"):
        a1, a3 = send(la, shift(dy=1)), send(la, shift(dy=-1))
        b1, b3 = send(lb, shift(dx=1)), send(lb, shift(dx=-1))
        theirs = send(lab, shift(dc=1))
        a1, a3, b1, b3, factor_one = lax.optimization_barrier((a1, a3, b1, b3, factor_one))
        *halves, whole = halves_of((a1, a3, b1, b3))
        moves = (shift(dy=1), shift(dy=-1), shift(dx=1), shift(dx=-1))
        halves = [send(v, m) for v, m in zip(halves, moves)]
        swapped = send(whole, shift(dc=1))
    with jax.named_scope("update"):
        first = [lab, theirs, a1, a3, b1, b3]
        modified = updated(FIRST, update_list, factor_one, panel_two, None, first, 40)
    with jax.named_scope("swap"):
        *halves, modified = lax.optimization_barrier((*halves, modified))
        halves = jnp.concatenate(halves)
        swapped_halves = send(halves, shift(dc=1))
    with jax.named_scope("factor_two"):
        second = [swapped, halves, swapped_halves]
        factor_two = updated(SECOND, update_list, factor_one, modified, full_two, second, 58)
    return factor_one, factor_two


def solution(mesh):
    return jax.shard_map(
        body,
        mesh=mesh,
        in_specs=(
            P(("row", "col"), None),
            P(("row", "col"), None),
            P(None, "col"),
            P(None, "col"),
            P(("row", "col"), None),
        ),
        out_specs=(P(("row", "col"), None), P(("row", "col"), None)),
        check_vma=False,
    )
```

```python
import jax
import jax.numpy as jnp
from jax import lax
from jax.experimental import pallas as pl
from jax.experimental.pallas import tpu as pltpu
from jax.sharding import PartitionSpec as P

SN = 2048
B = 256
ROWS = 512
KEEP = 1152
PIECE = 32
BF = jnp.bfloat16
F32 = jnp.float32
AXES = ("row", "col")
SIZES = (4, 4, 8, 2)
ANY = pl.BlockSpec(memory_space=pl.ANY)
SMEM = pl.BlockSpec(memory_space=pltpu.SMEM)
VMEM = pl.BlockSpec(memory_space=pltpu.VMEM)


def device(x, y, z, c):
    return (x * 4 + y) * 16 + z * 2 + c


def shift(dx=0, dy=0, dz=0, dc=0):
    pairs = []
    for x in range(4):
        for y in range(4):
            for z in range(8):
                for c in range(2):
                    to = device((x + dx) % 4, (y + dy) % 4, (z + dz) % 8, (c + dc) % 2)
                    pairs.append((device(x, y, z, c), to))
    return pairs


def along_z(moves):
    return [
        (r * 16 + a * 2 + c, r * 16 + b * 2 + c) for r in range(16) for a, b in moves for c in range(2)
    ]


def send(value, pairs):
    return lax.ppermute(value, AXES, pairs)


ORDER = (
    ((0, 0), (0, 1), (0, 2), (2, 1)),
    ((1, 0), (1, 1), (1, 3), (1, 2)),
    ((0, 3), (2, 3), (2, 2), (2, 0)),
    ((3, 0), (3, 1), (3, 3), (3, 2)),
)
NEAR = ((0, 1), (1, 0), (0, 3), (3, 0))


def in_plane(moves):
    return [(device(*a, 0, d), device(*b, 0, d)) for a, b in moves for d in range(4)]


MIRROR = [(r * 16 + c, r * 16 + 15 - c) for r in range(16) for c in range(9, 16)]


def tail_of(inverse):
    return inverse[KEEP:].reshape(7, 128, 128)[::-1].reshape(7 * 128, 128)


def packed(inverse, tail):
    return inverse[:KEEP] + jnp.concatenate([jnp.zeros((256, 128), BF), tail], axis=0)


def unpack_square(g, w, sems):
    for c in range(16):
        rows = ((c | 1) + 1) * 128
        pltpu.make_async_copy(
            g.at[pl.ds(c * SN, rows)], w.at[pl.ds(0, rows), pl.ds(c * 128, 128)], sems.at[c // 2]
        ).start()


def unpack(g, w, sems):
    for c in range(16):
        sem = sems.at[c // 2]
        count = (c | 1) + 1
        lead = min(count, 9)
        columns = pl.ds(c * 128, 128)
        pltpu.make_async_copy(
            g.at[pl.ds(c * KEEP, lead * 128)], w.at[pl.ds(0, lead * 128), columns], sem
        ).start()
        for h in range(9, count):
            pltpu.make_async_copy(
                g.at[pl.ds((15 - c) * KEEP + (17 - h) * 128, 128)],
                w.at[pl.ds(h * 128, 128), columns],
                sem,
            ).start()


def unpacked(w, sems, j):
    part = w.at[pl.ds(0, (j + 1) * 256), pl.ds(j * 256, 256)]
    pltpu.make_async_copy(part, part, sems.at[j]).wait()


def position():
    row, col = lax.axis_index("row"), lax.axis_index("col")
    return row // 4, row % 4, col // 2, col % 2


def pick_kernel(entries, panel, *refs):
    outs = refs[:4]
    rows, in_sems, sems = refs[4:]
    half_b = position()[2] > 0
    copies = []
    for j in range(2):
        start = pl.multiple_of(jnp.maximum(entries[0, j], 0) * B, B)
        copy = pltpu.make_async_copy(
            panel.at[pl.ds(start, B)], rows.at[pl.ds(j * B, B)], in_sems.at[j]
        )
        copy.start()
        copies.append(copy)
    for copy in copies:
        copy.wait()
    copies = []
    for k, group in enumerate(ORDER):
        for i, (x, y) in enumerate(group):
            start = jnp.where(half_b, 4 * x + y, 4 * y + x) * PIECE
            copy = pltpu.make_async_copy(
                rows.at[pl.ds(pl.multiple_of(start, PIECE), PIECE)],
                outs[k].at[pl.ds(i * PIECE, PIECE)],
                sems.at[k, i],
            )
            copy.start()
            copies.append(copy)
    for copy in copies:
        copy.wait()


def pick(entries, panel):
    return pl.pallas_call(
        pick_kernel,
        out_shape=[jax.ShapeDtypeStruct((4 * PIECE, SN), BF)] * 4,
        in_specs=[SMEM, ANY],
        out_specs=[ANY] * 4,
        scratch_shapes=[
            pltpu.VMEM((ROWS, SN), BF),
            pltpu.SemaphoreType.DMA((2,)),
            pltpu.SemaphoreType.DMA((4, 4)),
        ],
        compiler_params=pltpu.CompilerParams(vmem_limit_bytes=40 << 20),
        cost_estimate=pl.CostEstimate(flops=0, bytes_accessed=4 << 20, transcendentals=0),
    )(entries, panel)


def halves_kernel(*refs):
    ins, outs = refs[:4], refs[4:8]
    whole, rows, in_sems, sems, whole_sem = refs[8:]
    copies = []
    for k in range(4):
        copy = pltpu.make_async_copy(ins[k], rows.at[pl.ds(k * 128, 128)], in_sems.at[k])
        copy.start()
        copies.append(copy)
    for k in range(4):
        copies[k].wait()
        copy = pltpu.make_async_copy(
            rows.at[pl.ds(k * 128 + k % 2 * 64, 64)], outs[k], sems.at[k]
        )
        copy.start()
        copies.append(copy)
    copy = pltpu.make_async_copy(rows, whole, whole_sem)
    copy.start()
    copies.append(copy)
    for copy in copies[4:]:
        copy.wait()


def halves_of(arrays):
    return pl.pallas_call(
        halves_kernel,
        out_shape=[jax.ShapeDtypeStruct((64, SN), BF)] * 4 + [jax.ShapeDtypeStruct((512, SN), BF)],
        in_specs=[ANY] * 4,
        out_specs=[ANY] * 5,
        scratch_shapes=[
            pltpu.VMEM((512, SN), BF),
            pltpu.SemaphoreType.DMA((4,)),
            pltpu.SemaphoreType.DMA((4,)),
            pltpu.SemaphoreType.DMA,
        ],
        compiler_params=pltpu.CompilerParams(vmem_limit_bytes=8 << 20),
        cost_estimate=pl.CostEstimate(flops=0, bytes_accessed=5 << 20, transcendentals=0),
    )(*arrays)


def square_kernel(g, w, sems):
    unpack_square(g, w, sems)
    for j in range(8):
        unpacked(w, sems, j)


def square(gathered):
    return pl.pallas_call(
        square_kernel,
        out_shape=jax.ShapeDtypeStruct((SN, SN), BF),
        in_specs=[ANY],
        out_specs=VMEM,
        scratch_shapes=[pltpu.SemaphoreType.DMA((8,))],
        compiler_params=pltpu.CompilerParams(vmem_limit_bytes=40 << 20),
        cost_estimate=pl.CostEstimate(flops=0, bytes_accessed=13 << 20, transcendentals=0),
    )(gathered)


def panel_rows_kernel(*refs):
    ins, w, la, lb, lab, x, sems = refs[:8], *refs[8:]
    place = position()
    copies = []
    for k, ref in enumerate(ins):
        at = (k // 4) * 128 + ((place[k // 4] + 4 - k % 4) % 4) * PIECE
        copy = pltpu.make_async_copy(ref, x.at[pl.ds(pl.multiple_of(at, PIECE), PIECE)], sems.at[k])
        copy.start()
        copies.append(copy)
    for copy in copies:
        copy.wait()
    for j in range(8):
        columns = pl.ds(j * 256, 256)
        depth = (j + 1) * 256
        result = jnp.dot(
            x[:, pl.ds(0, depth)], w[pl.ds(0, depth), columns], preferred_element_type=F32
        ).astype(BF)
        lab[:, columns] = result
        la[:, columns] = result[:128]
        lb[:, columns] = result[128:]


def panel_rows(arrays, w):
    return pl.pallas_call(
        panel_rows_kernel,
        out_shape=[jax.ShapeDtypeStruct((n, SN), BF) for n in (128, 128, 256)],
        in_specs=[ANY] * 8 + [VMEM],
        out_specs=[VMEM] * 3,
        scratch_shapes=[pltpu.VMEM((256, SN), BF), pltpu.SemaphoreType.DMA((8,))],
        compiler_params=pltpu.CompilerParams(vmem_limit_bytes=16 << 20),
        cost_estimate=pl.CostEstimate(
            flops=256 * SN * SN, bytes_accessed=14 << 20, transcendentals=0
        ),
    )(*arrays, w)


def product_kernel(x, w, out, o, sems):
    copies = []
    for j in range(8):
        columns = pl.ds(j * 256, 256)
        depth = (j + 1) * 256
        o[:, columns] = jnp.dot(
            x[:, pl.ds(0, depth)], w[pl.ds(0, depth), columns], preferred_element_type=F32
        ).astype(BF)
        copy = pltpu.make_async_copy(o.at[:, columns], out.at[:, columns], sems.at[j])
        copy.start()
        copies.append(copy)
    for copy in copies:
        copy.wait()


def product(x, w):
    return pl.pallas_call(
        product_kernel,
        out_shape=jax.ShapeDtypeStruct((ROWS, SN), BF),
        in_specs=[VMEM, VMEM],
        out_specs=ANY,
        scratch_shapes=[pltpu.VMEM((ROWS, SN), BF), pltpu.SemaphoreType.DMA((8,))],
        compiler_params=pltpu.CompilerParams(vmem_limit_bytes=16 << 20),
        cost_estimate=pl.CostEstimate(
            flops=ROWS * SN * SN, bytes_accessed=12 << 20, transcendentals=0
        ),
    )(x, w)


def column_of(place, own, half, back):
    core = place[3] if own else 1 - place[3]
    coordinate = place[0] if half else place[1]
    return pl.multiple_of(((2 * half + core) * 4 + (coordinate + 4 - back) % 4) * 128, 128)


FIRST = (
    ((1, 0, 0), (1, 1, 0)),
    ((0, 0, 0), (0, 1, 0)),
    ((1, 0, 1), (1, 0, 3), (1, 1, 1), (1, 1, 3)),
)
SECOND = (
    ((0, 0, 1), (0, 0, 3), (0, 1, 1), (0, 1, 3)),
    ((1, 0, 2), (1, 1, 2)),
    ((0, 0, 2), (0, 1, 2)),
)


def subtract(parts, s, sources, m):
    place = position()
    for source, blocks in zip(sources, parts):
        for k in range(0, len(blocks), 2):
            update = lax.dot_general(
                s[...],
                source[pl.ds(k * 128, 256), :],
                (((1,), (1,)), ((), ())),
                preferred_element_type=F32,
            )
            for i in range(2):
                own = pl.ds(column_of(place, *blocks[k + i]), 128)
                m[:, own] = (m[:, own].astype(F32) - update[:, i * 128 : (i + 1) * 128]).astype(BF)


def first_kernel(entries, f1, panel, one, two, three, m, s, s_sems, m_sem):
    copies = []
    for j in range(2):
        start = pl.multiple_of(jnp.maximum(entries[0, j], 0) * B, B)
        copy = pltpu.make_async_copy(f1.at[pl.ds(start, B)], s.at[pl.ds(j * B, B)], s_sems.at[j])
        copy.start()
        copies.append(copy)
    copies.append(pltpu.make_async_copy(panel, m, m_sem))
    copies[-1].start()
    for copy in copies:
        copy.wait()
    for j in range(2):

        @pl.when(entries[0, j] < 0)
        def _(j=j):
            s[pl.ds(j * B, B), :] = jnp.zeros((B, SN), BF)

    subtract(FIRST, s, (one, two, three), m)


def first_update(entries, factor_one, panel, sources):
    return pl.pallas_call(
        first_kernel,
        out_shape=[jax.ShapeDtypeStruct((ROWS, SN), BF)] * 2,
        in_specs=[SMEM, ANY, ANY] + [VMEM] * 3,
        out_specs=[VMEM] * 2,
        scratch_shapes=[pltpu.SemaphoreType.DMA((2,)), pltpu.SemaphoreType.DMA],
        compiler_params=pltpu.CompilerParams(vmem_limit_bytes=16 << 20),
        cost_estimate=pl.CostEstimate(
            flops=ROWS * SN * SN, bytes_accessed=12 << 20, transcendentals=0
        ),
    )(entries, factor_one, panel, *sources)


def final_kernel(panel, s, one, two, three, g, out, m, w, o, m_sem, w_sems, o_sems):
    copy = pltpu.make_async_copy(panel, m, m_sem)
    copy.start()
    unpack(g, w, w_sems)
    copy.wait()
    subtract(SECOND, s, (one, two, three), m)
    for j in range(8):
        unpacked(w, w_sems, j)
    product_kernel(m, w, out, o, o_sems)


def final(modified, selected, sources, gathered):
    panel = pltpu.VMEM((ROWS, SN), BF)
    return pl.pallas_call(
        final_kernel,
        out_shape=jax.ShapeDtypeStruct((ROWS, SN), BF),
        in_specs=[ANY] + [VMEM] * 4 + [ANY],
        out_specs=ANY,
        scratch_shapes=[
            panel,
            pltpu.VMEM((SN, SN), BF),
            panel,
            pltpu.SemaphoreType.DMA,
            pltpu.SemaphoreType.DMA((8,)),
            pltpu.SemaphoreType.DMA((8,)),
        ],
        compiler_params=pltpu.CompilerParams(vmem_limit_bytes=50 << 20),
        cost_estimate=pl.CostEstimate(
            flops=2 * ROWS * SN * SN, bytes_accessed=18 << 20, transcendentals=0
        ),
    )(modified, selected, *sources, gathered)


def body(panel_one, panel_two, inverse_one, inverse_two, update_list):
    row, col = lax.axis_index("row"), lax.axis_index("col")
    z = col // 2

    with jax.named_scope("inverse_one"):
        full_one = lax.all_gather(inverse_one, "col", axis=0, tiled=True)

    with jax.named_scope("scatter_rows"):
        groups = pick(update_list, panel_one)
        parts = [send(groups[k], in_plane([((0, 0), NEAR[k])])) for k in range(4)]

    with jax.named_scope("forward_rows"):
        near = parts[0] + parts[1] + parts[2] + parts[3]
        kept = jnp.where(row == NEAR[0][1], near[32:64], near[:32])
        piece = jnp.where(row == 0, groups[0][:32], kept)
        for i in range(1, 4):
            moves = [(NEAR[k], ORDER[k][i]) for k in range(4) if NEAR[k] != ORDER[k][i]]
            piece = piece + send(near[i * 32 : (i + 1) * 32], in_plane(moves))

    with jax.named_scope("along_z"):
        piece = jnp.where(z < 2, piece, 0)
        piece = (
            piece
            + send(piece, along_z([(0, 2), (1, 3)]))
            + send(piece, along_z([(0, 6), (1, 7)]))
            + send(piece, along_z([(0, 4), (1, 5)]))
        )
        other = send(piece, along_z([(k, k ^ 1) for k in range(8)]))
        even = z % 2 == 0
        a, b = jnp.where(even, piece, other), jnp.where(even, other, piece)

    with jax.named_scope("inverse_two"):
        inverse_two, a, b = lax.optimization_barrier((inverse_two, a, b))
        tail = send(tail_of(inverse_two), MIRROR)

    with jax.named_scope("first_gather"):
        a_all = [a, send(a, shift(dx=1)), send(a, shift(dx=2)), send(a, shift(dx=-1))]
        b_all = [b, send(b, shift(dy=1)), send(b, shift(dy=2)), send(b, shift(dy=-1))]

    with jax.named_scope("inverse_two"):
        tail, *_ = lax.optimization_barrier((tail, *a_all, *b_all))
        full_two = lax.all_gather(packed(inverse_two, tail), "col", axis=0, tiled=True)

    with jax.named_scope("panel_rows"):
        whole_one = square(full_one)
        la, lb, lab = panel_rows(a_all + b_all, whole_one)

    with jax.named_scope("factor_one"):
        rows, _ = lax.optimization_barrier((panel_one, lab))
        factor_one = product(rows, whole_one)

    with jax.named_scope("second_gather"):
        a1, a3 = send(la, shift(dy=1)), send(la, shift(dy=-1))
        b1, b3 = send(lb, shift(dx=1)), send(lb, shift(dx=-1))
        theirs = send(lab, shift(dc=1))
        a1, a3, b1, b3, factor_one = lax.optimization_barrier((a1, a3, b1, b3, factor_one))
        *halves, whole = halves_of((a1, a3, b1, b3))
        moves = (shift(dy=1), shift(dy=-1), shift(dx=1), shift(dx=-1))
        halves = [send(v, m) for v, m in zip(halves, moves)]
        swapped = send(whole, shift(dc=1))
    with jax.named_scope("update"):
        modified, selected = first_update(update_list, factor_one, panel_two, (lab, theirs, whole))
    with jax.named_scope("swap"):
        *halves, modified = lax.optimization_barrier((*halves, modified))
        halves = jnp.concatenate(halves)
        swapped_halves = send(halves, shift(dc=1))
    with jax.named_scope("factor_two"):
        factor_two = final(modified, selected, (swapped, halves, swapped_halves), full_two)
    return factor_one, factor_two


def solution(mesh):
    return jax.shard_map(
        body,
        mesh=mesh,
        in_specs=(
            P(("row", "col"), None),
            P(("row", "col"), None),
            P(None, "col"),
            P(None, "col"),
            P(("row", "col"), None),
        ),
        out_specs=(P(("row", "col"), None), P(("row", "col"), None)),
        check_vma=False,
    )
```

```python
import jax
import jax.numpy as jnp
from jax import lax
from jax.experimental import pallas as pl
from jax.experimental.pallas import tpu as pltpu
from jax.sharding import PartitionSpec as P

SN = 2048
B = 256
ROWS = 512
KEEP = 1152
PIECE = 32
BF = jnp.bfloat16
F32 = jnp.float32
AXES = ("row", "col")
SIZES = (4, 4, 8, 2)
ANY = pl.BlockSpec(memory_space=pl.ANY)
SMEM = pl.BlockSpec(memory_space=pltpu.SMEM)
VMEM = pl.BlockSpec(memory_space=pltpu.VMEM)


def device(x, y, z, c):
    return (x * 4 + y) * 16 + z * 2 + c


def shift(dx=0, dy=0, dz=0, dc=0):
    pairs = []
    for x in range(4):
        for y in range(4):
            for z in range(8):
                for c in range(2):
                    to = device((x + dx) % 4, (y + dy) % 4, (z + dz) % 8, (c + dc) % 2)
                    pairs.append((device(x, y, z, c), to))
    return pairs


def along_z(moves):
    return [
        (r * 16 + a * 2 + c, r * 16 + b * 2 + c) for r in range(16) for a, b in moves for c in range(2)
    ]


def send(value, pairs):
    return lax.ppermute(value, AXES, pairs)


ORDER = (
    ((0, 0), (0, 1), (0, 2), (2, 1)),
    ((1, 0), (1, 1), (1, 3), (1, 2)),
    ((0, 3), (2, 3), (2, 2), (2, 0)),
    ((3, 0), (3, 1), (3, 3), (3, 2)),
)
NEAR = ((0, 1), (1, 0), (0, 3), (3, 0))


def in_plane(moves):
    return [(device(*a, 0, d), device(*b, 0, d)) for a, b in moves for d in range(4)]


MIRROR = [(r * 16 + c, r * 16 + 15 - c) for r in range(16) for c in range(9, 16)]


def tail_of(inverse):
    return inverse[KEEP:].reshape(7, 128, 128)[::-1].reshape(7 * 128, 128)


def packed(inverse, tail):
    return inverse[:KEEP] + jnp.concatenate([jnp.zeros((256, 128), BF), tail], axis=0)


def unpack_square(g, w, sems):
    for c in range(16):
        rows = ((c | 1) + 1) * 128
        pltpu.make_async_copy(
            g.at[pl.ds(c * SN, rows)], w.at[pl.ds(0, rows), pl.ds(c * 128, 128)], sems.at[c // 2]
        ).start()


def unpack(g, w, sems):
    for c in range(16):
        sem = sems.at[c // 2]
        count = (c | 1) + 1
        lead = min(count, 9)
        columns = pl.ds(c * 128, 128)
        pltpu.make_async_copy(
            g.at[pl.ds(c * KEEP, lead * 128)], w.at[pl.ds(0, lead * 128), columns], sem
        ).start()
        for h in range(9, count):
            pltpu.make_async_copy(
                g.at[pl.ds((15 - c) * KEEP + (17 - h) * 128, 128)],
                w.at[pl.ds(h * 128, 128), columns],
                sem,
            ).start()


def unpacked(w, sems, j):
    part = w.at[pl.ds(0, (j + 1) * 256), pl.ds(j * 256, 256)]
    pltpu.make_async_copy(part, part, sems.at[j]).wait()


def position():
    row, col = lax.axis_index("row"), lax.axis_index("col")
    return row // 4, row % 4, col // 2, col % 2


def pick_kernel(entries, panel, *refs):
    outs = refs[:4]
    rows, in_sems, sems = refs[4:]
    half_b = position()[2] > 0
    copies = []
    for j in range(2):
        start = pl.multiple_of(jnp.maximum(entries[0, j], 0) * B, B)
        copy = pltpu.make_async_copy(
            panel.at[pl.ds(start, B)], rows.at[pl.ds(j * B, B)], in_sems.at[j]
        )
        copy.start()
        copies.append(copy)
    for copy in copies:
        copy.wait()
    copies = []
    for k, group in enumerate(ORDER):
        for i, (x, y) in enumerate(group):
            start = jnp.where(half_b, 4 * x + y, 4 * y + x) * PIECE
            copy = pltpu.make_async_copy(
                rows.at[pl.ds(pl.multiple_of(start, PIECE), PIECE)],
                outs[k].at[pl.ds(i * PIECE, PIECE)],
                sems.at[k, i],
            )
            copy.start()
            copies.append(copy)
    for copy in copies:
        copy.wait()


def pick(entries, panel):
    return pl.pallas_call(
        pick_kernel,
        out_shape=[jax.ShapeDtypeStruct((4 * PIECE, SN), BF)] * 4,
        in_specs=[SMEM, ANY],
        out_specs=[ANY] * 4,
        scratch_shapes=[
            pltpu.VMEM((ROWS, SN), BF),
            pltpu.SemaphoreType.DMA((2,)),
            pltpu.SemaphoreType.DMA((4, 4)),
        ],
        compiler_params=pltpu.CompilerParams(vmem_limit_bytes=40 << 20),
        cost_estimate=pl.CostEstimate(flops=0, bytes_accessed=4 << 20, transcendentals=0),
    )(entries, panel)


def halves_kernel(*refs):
    ins, outs = refs[:4], refs[4:8]
    whole, rows, in_sems, sems, whole_sem = refs[8:]
    copies = []
    for k in range(4):
        copy = pltpu.make_async_copy(ins[k], rows.at[pl.ds(k * 128, 128)], in_sems.at[k])
        copy.start()
        copies.append(copy)
    for k in range(4):
        copies[k].wait()
        copy = pltpu.make_async_copy(
            rows.at[pl.ds(k * 128 + k % 2 * 64, 64)], outs[k], sems.at[k]
        )
        copy.start()
        copies.append(copy)
    copy = pltpu.make_async_copy(rows, whole, whole_sem)
    copy.start()
    copies.append(copy)
    for copy in copies[4:]:
        copy.wait()


def halves_of(arrays):
    return pl.pallas_call(
        halves_kernel,
        out_shape=[jax.ShapeDtypeStruct((64, SN), BF)] * 4 + [jax.ShapeDtypeStruct((512, SN), BF)],
        in_specs=[ANY] * 4,
        out_specs=[ANY] * 5,
        scratch_shapes=[
            pltpu.VMEM((512, SN), BF),
            pltpu.SemaphoreType.DMA((4,)),
            pltpu.SemaphoreType.DMA((4,)),
            pltpu.SemaphoreType.DMA,
        ],
        compiler_params=pltpu.CompilerParams(vmem_limit_bytes=8 << 20),
        cost_estimate=pl.CostEstimate(flops=0, bytes_accessed=5 << 20, transcendentals=0),
    )(*arrays)


def square_kernel(g, w, sems):
    unpack_square(g, w, sems)
    for j in range(8):
        unpacked(w, sems, j)


def square(gathered):
    return pl.pallas_call(
        square_kernel,
        out_shape=jax.ShapeDtypeStruct((SN, SN), BF),
        in_specs=[ANY],
        out_specs=VMEM,
        scratch_shapes=[pltpu.SemaphoreType.DMA((8,))],
        compiler_params=pltpu.CompilerParams(vmem_limit_bytes=40 << 20),
        cost_estimate=pl.CostEstimate(flops=0, bytes_accessed=13 << 20, transcendentals=0),
    )(gathered)


def panel_rows_kernel(*refs):
    ins, w, la, lb, lab, x, sems = refs[:8], *refs[8:]
    place = position()
    copies = []
    for k, ref in enumerate(ins):
        at = (k // 4) * 128 + ((place[k // 4] + 4 - k % 4) % 4) * PIECE
        copy = pltpu.make_async_copy(ref, x.at[pl.ds(pl.multiple_of(at, PIECE), PIECE)], sems.at[k])
        copy.start()
        copies.append(copy)
    for copy in copies:
        copy.wait()
    for j in range(8):
        columns = pl.ds(j * 256, 256)
        depth = (j + 1) * 256
        result = jnp.dot(
            x[:, pl.ds(0, depth)], w[pl.ds(0, depth), columns], preferred_element_type=F32
        ).astype(BF)
        lab[:, columns] = result
        la[:, columns] = result[:128]
        lb[:, columns] = result[128:]


def panel_rows(arrays, w):
    return pl.pallas_call(
        panel_rows_kernel,
        out_shape=[jax.ShapeDtypeStruct((n, SN), BF) for n in (128, 128, 256)],
        in_specs=[ANY] * 8 + [VMEM],
        out_specs=[VMEM] * 3,
        scratch_shapes=[pltpu.VMEM((256, SN), BF), pltpu.SemaphoreType.DMA((8,))],
        compiler_params=pltpu.CompilerParams(vmem_limit_bytes=16 << 20),
        cost_estimate=pl.CostEstimate(
            flops=256 * SN * SN, bytes_accessed=14 << 20, transcendentals=0
        ),
    )(*arrays, w)


def product_kernel(x, w, out, o, sems):
    copies = []
    for j in range(8):
        columns = pl.ds(j * 256, 256)
        depth = (j + 1) * 256
        o[:, columns] = jnp.dot(
            x[:, pl.ds(0, depth)], w[pl.ds(0, depth), columns], preferred_element_type=F32
        ).astype(BF)
        copy = pltpu.make_async_copy(o.at[:, columns], out.at[:, columns], sems.at[j])
        copy.start()
        copies.append(copy)
    for copy in copies:
        copy.wait()


def product(x, w):
    return pl.pallas_call(
        product_kernel,
        out_shape=jax.ShapeDtypeStruct((ROWS, SN), BF),
        in_specs=[VMEM, VMEM],
        out_specs=ANY,
        scratch_shapes=[pltpu.VMEM((ROWS, SN), BF), pltpu.SemaphoreType.DMA((8,))],
        compiler_params=pltpu.CompilerParams(vmem_limit_bytes=16 << 20),
        cost_estimate=pl.CostEstimate(
            flops=ROWS * SN * SN, bytes_accessed=12 << 20, transcendentals=0
        ),
    )(x, w)


def column_of(place, own, half, back):
    core = place[3] if own else 1 - place[3]
    coordinate = place[0] if half else place[1]
    return pl.multiple_of(((2 * half + core) * 4 + (coordinate + 4 - back) % 4) * 128, 128)


FIRST = (
    ((1, 0, 0), (1, 1, 0)),
    ((0, 0, 0), (0, 1, 0)),
    ((1, 0, 1), (1, 0, 3), (1, 1, 1), (1, 1, 3)),
)
SECOND = (
    ((0, 0, 1), (0, 0, 3), (0, 1, 1), (0, 1, 3)),
    ((1, 0, 2), (1, 1, 2)),
    ((0, 0, 2), (0, 1, 2)),
)


def subtract(parts, s, sources, old, new):
    place = position()
    for source, blocks in zip(sources, parts):
        for k in range(0, len(blocks), 2):
            update = lax.dot_general(
                s[...],
                source[pl.ds(k * 128, 256), :],
                (((1,), (1,)), ((), ())),
                preferred_element_type=F32,
            )
            for i in range(2):
                own = pl.ds(column_of(place, *blocks[k + i]), 128)
                part = update[:, i * 128 : (i + 1) * 128]
                new[:, own] = (old[:, own].astype(F32) - part).astype(BF)


def first_kernel(entries, f1, panel, one, two, three, m, s, s_sems, m_sem):
    copies = []
    for j in range(2):
        start = pl.multiple_of(jnp.maximum(entries[0, j], 0) * B, B)
        copy = pltpu.make_async_copy(f1.at[pl.ds(start, B)], s.at[pl.ds(j * B, B)], s_sems.at[j])
        copy.start()
        copies.append(copy)
    copies.append(pltpu.make_async_copy(panel, m, m_sem))
    copies[-1].start()
    for copy in copies:
        copy.wait()
    for j in range(2):

        @pl.when(entries[0, j] < 0)
        def _(j=j):
            s[pl.ds(j * B, B), :] = jnp.zeros((B, SN), BF)

    subtract(FIRST, s, (one, two, three), m, m)


def first_update(entries, factor_one, panel, sources):
    return pl.pallas_call(
        first_kernel,
        out_shape=[jax.ShapeDtypeStruct((ROWS, SN), BF)] * 2,
        in_specs=[SMEM, ANY, ANY] + [VMEM] * 3,
        out_specs=[VMEM] * 2,
        scratch_shapes=[pltpu.SemaphoreType.DMA((2,)), pltpu.SemaphoreType.DMA],
        compiler_params=pltpu.CompilerParams(vmem_limit_bytes=16 << 20),
        cost_estimate=pl.CostEstimate(
            flops=ROWS * SN * SN, bytes_accessed=12 << 20, transcendentals=0
        ),
    )(entries, factor_one, panel, *sources)


def second_kernel(old, s, one, two, three, new):
    place = position()
    subtract(SECOND, s, (one, two, three), old, new)
    for blocks in FIRST:
        for block in blocks:
            own = pl.ds(column_of(place, *block), 128)
            new[:, own] = old[:, own]


def second_update(modified, selected, sources):
    return pl.pallas_call(
        second_kernel,
        out_shape=jax.ShapeDtypeStruct((ROWS, SN), BF),
        in_specs=[VMEM] * 5,
        out_specs=VMEM,
        compiler_params=pltpu.CompilerParams(vmem_limit_bytes=16 << 20),
        cost_estimate=pl.CostEstimate(
            flops=ROWS * SN * SN, bytes_accessed=12 << 20, transcendentals=0
        ),
    )(modified, selected, *sources)


def final_kernel(m, g, out, w, o, w_sems, o_sems):
    unpack(g, w, w_sems)
    for j in range(8):
        unpacked(w, w_sems, j)
    product_kernel(m, w, out, o, o_sems)


def final(modified, gathered):
    return pl.pallas_call(
        final_kernel,
        out_shape=jax.ShapeDtypeStruct((ROWS, SN), BF),
        in_specs=[VMEM, ANY],
        out_specs=ANY,
        scratch_shapes=[
            pltpu.VMEM((SN, SN), BF),
            pltpu.VMEM((ROWS, SN), BF),
            pltpu.SemaphoreType.DMA((8,)),
            pltpu.SemaphoreType.DMA((8,)),
        ],
        compiler_params=pltpu.CompilerParams(vmem_limit_bytes=50 << 20),
        cost_estimate=pl.CostEstimate(
            flops=ROWS * SN * SN, bytes_accessed=9 << 20, transcendentals=0
        ),
    )(modified, gathered)


def body(panel_one, panel_two, inverse_one, inverse_two, update_list):
    row, col = lax.axis_index("row"), lax.axis_index("col")
    z = col // 2

    with jax.named_scope("inverse_one"):
        full_one = lax.all_gather(inverse_one, "col", axis=0, tiled=True)

    with jax.named_scope("scatter_rows"):
        groups = pick(update_list, panel_one)
        parts = [send(groups[k], in_plane([((0, 0), NEAR[k])])) for k in range(4)]

    with jax.named_scope("forward_rows"):
        near = parts[0] + parts[1] + parts[2] + parts[3]
        kept = jnp.where(row == NEAR[0][1], near[32:64], near[:32])
        piece = jnp.where(row == 0, groups[0][:32], kept)
        for i in range(1, 4):
            moves = [(NEAR[k], ORDER[k][i]) for k in range(4) if NEAR[k] != ORDER[k][i]]
            piece = piece + send(near[i * 32 : (i + 1) * 32], in_plane(moves))

    with jax.named_scope("along_z"):
        piece = jnp.where(z < 2, piece, 0)
        piece = (
            piece
            + send(piece, along_z([(0, 2), (1, 3)]))
            + send(piece, along_z([(0, 6), (1, 7)]))
            + send(piece, along_z([(0, 4), (1, 5)]))
        )
        other = send(piece, along_z([(k, k ^ 1) for k in range(8)]))
        even = z % 2 == 0
        a, b = jnp.where(even, piece, other), jnp.where(even, other, piece)

    with jax.named_scope("inverse_two"):
        inverse_two, a, b = lax.optimization_barrier((inverse_two, a, b))
        tail = send(tail_of(inverse_two), MIRROR)

    with jax.named_scope("first_gather"):
        a_all = [a, send(a, shift(dx=1)), send(a, shift(dx=2)), send(a, shift(dx=-1))]
        b_all = [b, send(b, shift(dy=1)), send(b, shift(dy=2)), send(b, shift(dy=-1))]

    with jax.named_scope("inverse_two"):
        tail, *_ = lax.optimization_barrier((tail, *a_all, *b_all))
        full_two = lax.all_gather(packed(inverse_two, tail), "col", axis=0, tiled=True)

    with jax.named_scope("panel_rows"):
        whole_one = square(full_one)
        la, lb, lab = panel_rows(a_all + b_all, whole_one)

    with jax.named_scope("factor_one"):
        rows, _ = lax.optimization_barrier((panel_one, lab))
        factor_one = product(rows, whole_one)

    with jax.named_scope("second_gather"):
        a1, a3 = send(la, shift(dy=1)), send(la, shift(dy=-1))
        b1, b3 = send(lb, shift(dx=1)), send(lb, shift(dx=-1))
        theirs = send(lab, shift(dc=1))
        a1, a3, b1, b3, factor_one = lax.optimization_barrier((a1, a3, b1, b3, factor_one))
        *halves, whole = halves_of((a1, a3, b1, b3))
        moves = (shift(dy=1), shift(dy=-1), shift(dx=1), shift(dx=-1))
        halves = [send(v, m) for v, m in zip(halves, moves)]
        swapped = send(whole, shift(dc=1))
    with jax.named_scope("update"):
        modified, selected = first_update(update_list, factor_one, panel_two, (lab, theirs, whole))
    with jax.named_scope("swap"):
        *halves, modified = lax.optimization_barrier((*halves, modified))
        halves = jnp.concatenate(halves)
        swapped_halves = send(halves, shift(dc=1))
        modified = second_update(modified, selected, (swapped, halves, swapped_halves))
    with jax.named_scope("factor_two"):
        factor_two = final(modified, full_two)
    return factor_one, factor_two


def solution(mesh):
    return jax.shard_map(
        body,
        mesh=mesh,
        in_specs=(
            P(("row", "col"), None),
            P(("row", "col"), None),
            P(None, "col"),
            P(None, "col"),
            P(("row", "col"), None),
        ),
        out_specs=(P(("row", "col"), None), P(("row", "col"), None)),
        check_vma=False,
    )
```

```python
import jax
import jax.numpy as jnp
from jax import lax
from jax.experimental import pallas as pl
from jax.experimental.pallas import tpu as pltpu
from jax.sharding import PartitionSpec as P

SN = 2048
B = 256
ROWS = 512
KEEP = 1152
PIECE = 32
BF = jnp.bfloat16
F32 = jnp.float32
AXES = ("row", "col")
SIZES = (4, 4, 8, 2)
ANY = pl.BlockSpec(memory_space=pl.ANY)
SMEM = pl.BlockSpec(memory_space=pltpu.SMEM)
VMEM = pl.BlockSpec(memory_space=pltpu.VMEM)


def device(x, y, z, c):
    return (x * 4 + y) * 16 + z * 2 + c


def shift(dx=0, dy=0, dz=0, dc=0):
    pairs = []
    for x in range(4):
        for y in range(4):
            for z in range(8):
                for c in range(2):
                    to = device((x + dx) % 4, (y + dy) % 4, (z + dz) % 8, (c + dc) % 2)
                    pairs.append((device(x, y, z, c), to))
    return pairs


def along_z(moves):
    return [
        (r * 16 + a * 2 + c, r * 16 + b * 2 + c) for r in range(16) for a, b in moves for c in range(2)
    ]


def send(value, pairs):
    return lax.ppermute(value, AXES, pairs)


ORDER = (
    ((0, 0), (0, 1), (0, 2), (2, 1)),
    ((1, 0), (1, 1), (1, 3), (1, 2)),
    ((0, 3), (2, 3), (2, 2), (2, 0)),
    ((3, 0), (3, 1), (3, 3), (3, 2)),
)
NEAR = ((0, 1), (1, 0), (0, 3), (3, 0))


def in_plane(moves):
    return [(device(*a, 0, d), device(*b, 0, d)) for a, b in moves for d in range(4)]


MIRROR = [(r * 16 + c, r * 16 + 15 - c) for r in range(16) for c in range(9, 16)]


def tail_of(inverse):
    return inverse[KEEP:].reshape(7, 128, 128)[::-1].reshape(7 * 128, 128)


def packed(inverse, tail):
    return inverse[:KEEP] + jnp.concatenate([jnp.zeros((256, 128), BF), tail], axis=0)


def unpack_square(g, w, sems):
    for c in range(16):
        rows = ((c | 1) + 1) * 128
        pltpu.make_async_copy(
            g.at[pl.ds(c * SN, rows)], w.at[pl.ds(0, rows), pl.ds(c * 128, 128)], sems.at[c // 2]
        ).start()


def unpack(g, w, sems):
    for c in range(16):
        sem = sems.at[c // 2]
        count = (c | 1) + 1
        lead = min(count, 9)
        columns = pl.ds(c * 128, 128)
        pltpu.make_async_copy(
            g.at[pl.ds(c * KEEP, lead * 128)], w.at[pl.ds(0, lead * 128), columns], sem
        ).start()
        for h in range(9, count):
            pltpu.make_async_copy(
                g.at[pl.ds((15 - c) * KEEP + (17 - h) * 128, 128)],
                w.at[pl.ds(h * 128, 128), columns],
                sem,
            ).start()


def unpacked(w, sems, j):
    part = w.at[pl.ds(0, (j + 1) * 256), pl.ds(j * 256, 256)]
    pltpu.make_async_copy(part, part, sems.at[j]).wait()


def position():
    row, col = lax.axis_index("row"), lax.axis_index("col")
    return row // 4, row % 4, col // 2, col % 2


def pick_kernel(entries, panel, *refs):
    outs = refs[:4]
    rows, in_sems, sems = refs[4:]
    half_b = position()[2] > 0
    copies = []
    for j in range(2):
        start = pl.multiple_of(jnp.maximum(entries[0, j], 0) * B, B)
        copy = pltpu.make_async_copy(
            panel.at[pl.ds(start, B)], rows.at[pl.ds(j * B, B)], in_sems.at[j]
        )
        copy.start()
        copies.append(copy)
    for copy in copies:
        copy.wait()
    copies = []
    for k, group in enumerate(ORDER):
        for i, (x, y) in enumerate(group):
            start = jnp.where(half_b, 4 * x + y, 4 * y + x) * PIECE
            copy = pltpu.make_async_copy(
                rows.at[pl.ds(pl.multiple_of(start, PIECE), PIECE)],
                outs[k].at[pl.ds(i * PIECE, PIECE)],
                sems.at[k, i],
            )
            copy.start()
            copies.append(copy)
    for copy in copies:
        copy.wait()


def pick(entries, panel):
    return pl.pallas_call(
        pick_kernel,
        out_shape=[jax.ShapeDtypeStruct((4 * PIECE, SN), BF)] * 4,
        in_specs=[SMEM, ANY],
        out_specs=[ANY] * 4,
        scratch_shapes=[
            pltpu.VMEM((ROWS, SN), BF),
            pltpu.SemaphoreType.DMA((2,)),
            pltpu.SemaphoreType.DMA((4, 4)),
        ],
        compiler_params=pltpu.CompilerParams(vmem_limit_bytes=40 << 20),
        cost_estimate=pl.CostEstimate(flops=0, bytes_accessed=4 << 20, transcendentals=0),
    )(entries, panel)


def halves_kernel(*refs):
    ins, outs = refs[:5], refs[5:9]
    whole, rows, in_sems, sems, whole_sem = refs[9:]
    copies = []
    for k in range(5):
        copy = pltpu.make_async_copy(
            ins[k], rows.at[pl.ds(k * 128, 256 if k == 4 else 128)], in_sems.at[k]
        )
        copy.start()
        copies.append(copy)
    for k in range(4):
        copies[k].wait()
        copy = pltpu.make_async_copy(
            rows.at[pl.ds(k * 128 + k % 2 * 64, 64)], outs[k], sems.at[k]
        )
        copy.start()
        copies.append(copy)
    copies[4].wait()
    copy = pltpu.make_async_copy(rows, whole, whole_sem)
    copy.start()
    copies.append(copy)
    for copy in copies[5:]:
        copy.wait()


def halves_of(arrays):
    return pl.pallas_call(
        halves_kernel,
        out_shape=[jax.ShapeDtypeStruct((64, SN), BF)] * 4 + [jax.ShapeDtypeStruct((768, SN), BF)],
        in_specs=[ANY] * 5,
        out_specs=[ANY] * 5,
        scratch_shapes=[
            pltpu.VMEM((768, SN), BF),
            pltpu.SemaphoreType.DMA((5,)),
            pltpu.SemaphoreType.DMA((4,)),
            pltpu.SemaphoreType.DMA,
        ],
        compiler_params=pltpu.CompilerParams(vmem_limit_bytes=8 << 20),
        cost_estimate=pl.CostEstimate(flops=0, bytes_accessed=5 << 20, transcendentals=0),
    )(*arrays)


def square_kernel(g, w, sems):
    unpack_square(g, w, sems)
    for j in range(8):
        unpacked(w, sems, j)


def square(gathered):
    return pl.pallas_call(
        square_kernel,
        out_shape=jax.ShapeDtypeStruct((SN, SN), BF),
        in_specs=[ANY],
        out_specs=VMEM,
        scratch_shapes=[pltpu.SemaphoreType.DMA((8,))],
        compiler_params=pltpu.CompilerParams(vmem_limit_bytes=40 << 20),
        cost_estimate=pl.CostEstimate(flops=0, bytes_accessed=13 << 20, transcendentals=0),
    )(gathered)


def panel_rows_kernel(*refs):
    ins, w, la, lb, lab, x, sems = refs[:8], *refs[8:]
    place = position()
    copies = []
    for k, ref in enumerate(ins):
        at = (k // 4) * 128 + ((place[k // 4] + 4 - k % 4) % 4) * PIECE
        copy = pltpu.make_async_copy(ref, x.at[pl.ds(pl.multiple_of(at, PIECE), PIECE)], sems.at[k])
        copy.start()
        copies.append(copy)
    for copy in copies:
        copy.wait()
    for j in range(8):
        columns = pl.ds(j * 256, 256)
        depth = (j + 1) * 256
        result = jnp.dot(
            x[:, pl.ds(0, depth)], w[pl.ds(0, depth), columns], preferred_element_type=F32
        ).astype(BF)
        lab[:, columns] = result
        la[:, columns] = result[:128]
        lb[:, columns] = result[128:]


def panel_rows(arrays, w):
    return pl.pallas_call(
        panel_rows_kernel,
        out_shape=[jax.ShapeDtypeStruct((n, SN), BF) for n in (128, 128, 256)],
        in_specs=[ANY] * 8 + [VMEM],
        out_specs=[VMEM] * 3,
        scratch_shapes=[pltpu.VMEM((256, SN), BF), pltpu.SemaphoreType.DMA((8,))],
        compiler_params=pltpu.CompilerParams(vmem_limit_bytes=16 << 20),
        cost_estimate=pl.CostEstimate(
            flops=256 * SN * SN, bytes_accessed=14 << 20, transcendentals=0
        ),
    )(*arrays, w)


def product_kernel(x, w, out, o, sems, w_sems=None):
    copies = []
    for j in range(8):
        if w_sems is not None and j in (0, 5):
            for k in range(0, 5) if j == 0 else range(5, 8):
                unpacked(w, w_sems, k)
        columns = pl.ds(j * 256, 256)
        depth = (j + 1) * 256
        o[:, columns] = jnp.dot(
            x[:, pl.ds(0, depth)], w[pl.ds(0, depth), columns], preferred_element_type=F32
        ).astype(BF)
        copy = pltpu.make_async_copy(o.at[:, columns], out.at[:, columns], sems.at[j])
        copy.start()
        copies.append(copy)
    for copy in copies:
        copy.wait()


def product(x, w):
    return pl.pallas_call(
        product_kernel,
        out_shape=jax.ShapeDtypeStruct((ROWS, SN), BF),
        in_specs=[VMEM, VMEM],
        out_specs=ANY,
        scratch_shapes=[pltpu.VMEM((ROWS, SN), BF), pltpu.SemaphoreType.DMA((8,))],
        compiler_params=pltpu.CompilerParams(vmem_limit_bytes=16 << 20),
        cost_estimate=pl.CostEstimate(
            flops=ROWS * SN * SN, bytes_accessed=12 << 20, transcendentals=0
        ),
    )(x, w)


def column_of(place, own, half, back):
    core = place[3] if own else 1 - place[3]
    coordinate = place[0] if half else place[1]
    return pl.multiple_of(((2 * half + core) * 4 + (coordinate + 4 - back) % 4) * 128, 128)


FIRST = (((1, 0, 1), (1, 0, 3), (1, 1, 1), (1, 1, 3), (1, 0, 0), (1, 1, 0)),)
SECOND = (
    ((0, 0, 1), (0, 0, 3), (0, 1, 1), (0, 1, 3), (0, 0, 0), (0, 1, 0)),
    ((1, 0, 2), (1, 1, 2)),
    ((0, 0, 2), (0, 1, 2)),
)


def subtract(parts, s, sources, old, new):
    place = position()
    for source, blocks in zip(sources, parts):
        for k in range(0, len(blocks), 2):
            update = lax.dot_general(
                s[...],
                source[pl.ds(k * 128, 256), :],
                (((1,), (1,)), ((), ())),
                preferred_element_type=F32,
            )
            for i in range(2):
                own = pl.ds(column_of(place, *blocks[k + i]), 128)
                part = update[:, i * 128 : (i + 1) * 128]
                new[:, own] = (old[:, own].astype(F32) - part).astype(BF)


def first_kernel(entries, f1, panel, own, m, s, s_sems, m_sem):
    copies = []
    for j in range(2):
        start = pl.multiple_of(jnp.maximum(entries[0, j], 0) * B, B)
        copy = pltpu.make_async_copy(f1.at[pl.ds(start, B)], s.at[pl.ds(j * B, B)], s_sems.at[j])
        copy.start()
        copies.append(copy)
    copies.append(pltpu.make_async_copy(panel, m, m_sem))
    copies[-1].start()
    for copy in copies:
        copy.wait()
    for j in range(2):

        @pl.when(entries[0, j] < 0)
        def _(j=j):
            s[pl.ds(j * B, B), :] = jnp.zeros((B, SN), BF)

    subtract(FIRST, s, (own,), m, m)


def first_update(entries, factor_one, panel, own):
    return pl.pallas_call(
        first_kernel,
        out_shape=[jax.ShapeDtypeStruct((ROWS, SN), BF)] * 2,
        in_specs=[SMEM, ANY, ANY, VMEM],
        out_specs=[VMEM] * 2,
        scratch_shapes=[pltpu.SemaphoreType.DMA((2,)), pltpu.SemaphoreType.DMA],
        compiler_params=pltpu.CompilerParams(vmem_limit_bytes=16 << 20),
        cost_estimate=pl.CostEstimate(
            flops=ROWS * SN * SN, bytes_accessed=12 << 20, transcendentals=0
        ),
    )(entries, factor_one, panel, own)


def second_kernel(old, s, one, two, three, new):
    place = position()
    subtract(SECOND, s, (one, two, three), old, new)
    for blocks in FIRST:
        for block in blocks:
            own = pl.ds(column_of(place, *block), 128)
            new[:, own] = old[:, own]


def second_update(modified, selected, sources):
    return pl.pallas_call(
        second_kernel,
        out_shape=jax.ShapeDtypeStruct((ROWS, SN), BF),
        in_specs=[VMEM] * 5,
        out_specs=VMEM,
        compiler_params=pltpu.CompilerParams(vmem_limit_bytes=16 << 20),
        cost_estimate=pl.CostEstimate(
            flops=ROWS * SN * SN, bytes_accessed=12 << 20, transcendentals=0
        ),
    )(modified, selected, *sources)


def final_kernel(m, g, out, w, o, w_sems, o_sems):
    unpack(g, w, w_sems)
    product_kernel(m, w, out, o, o_sems, w_sems)


def final(modified, gathered):
    return pl.pallas_call(
        final_kernel,
        out_shape=jax.ShapeDtypeStruct((ROWS, SN), BF),
        in_specs=[VMEM, ANY],
        out_specs=ANY,
        scratch_shapes=[
            pltpu.VMEM((SN, SN), BF),
            pltpu.VMEM((ROWS, SN), BF),
            pltpu.SemaphoreType.DMA((8,)),
            pltpu.SemaphoreType.DMA((8,)),
        ],
        compiler_params=pltpu.CompilerParams(vmem_limit_bytes=50 << 20),
        cost_estimate=pl.CostEstimate(
            flops=ROWS * SN * SN, bytes_accessed=9 << 20, transcendentals=0
        ),
    )(modified, gathered)


def body(panel_one, panel_two, inverse_one, inverse_two, update_list):
    row, col = lax.axis_index("row"), lax.axis_index("col")
    z = col // 2

    with jax.named_scope("inverse_one"):
        full_one = lax.all_gather(inverse_one, "col", axis=0, tiled=True)

    with jax.named_scope("scatter_rows"):
        groups = pick(update_list, panel_one)
        parts = [send(groups[k], in_plane([((0, 0), NEAR[k])])) for k in range(4)]

    with jax.named_scope("forward_rows"):
        near = parts[0] + parts[1] + parts[2] + parts[3]
        kept = jnp.where(row == NEAR[0][1], near[32:64], near[:32])
        piece = jnp.where(row == 0, groups[0][:32], kept)
        for i in range(1, 4):
            moves = [(NEAR[k], ORDER[k][i]) for k in range(4) if NEAR[k] != ORDER[k][i]]
            piece = piece + send(near[i * 32 : (i + 1) * 32], in_plane(moves))

    with jax.named_scope("along_z"):
        piece = jnp.where(z < 2, piece, 0)
        piece = (
            piece
            + send(piece, along_z([(0, 2), (1, 3)]))
            + send(piece, along_z([(0, 6), (1, 7)]))
            + send(piece, along_z([(0, 4), (1, 5)]))
        )
        other = send(piece, along_z([(k, k ^ 1) for k in range(8)]))
        even = z % 2 == 0
        a, b = jnp.where(even, piece, other), jnp.where(even, other, piece)

    with jax.named_scope("inverse_two"):
        inverse_two, a, b = lax.optimization_barrier((inverse_two, a, b))
        tail = send(tail_of(inverse_two), MIRROR)

    with jax.named_scope("first_gather"):
        a_all = [a, send(a, shift(dx=1)), send(a, shift(dx=2)), send(a, shift(dx=-1))]
        b_all = [b, send(b, shift(dy=1)), send(b, shift(dy=2)), send(b, shift(dy=-1))]

    with jax.named_scope("inverse_two"):
        tail, *_ = lax.optimization_barrier((tail, *a_all, *b_all))
        full_two = lax.all_gather(packed(inverse_two, tail), "col", axis=0, tiled=True)

    with jax.named_scope("panel_rows"):
        whole_one = square(full_one)
        la, lb, lab = panel_rows(a_all + b_all, whole_one)

    with jax.named_scope("factor_one"):
        rows, _ = lax.optimization_barrier((panel_one, lab))
        factor_one = product(rows, whole_one)

    with jax.named_scope("second_gather"):
        a1, a3 = send(la, shift(dy=1)), send(la, shift(dy=-1))
        b1, b3 = send(lb, shift(dx=1)), send(lb, shift(dx=-1))
        a1, a3, b1, b3, factor_one = lax.optimization_barrier((a1, a3, b1, b3, factor_one))
        *halves, whole = halves_of((a1, a3, b1, b3, lab))
        moves = (shift(dy=1), shift(dy=-1), shift(dx=1), shift(dx=-1))
        halves = [send(v, m) for v, m in zip(halves, moves)]
        swapped = send(whole, shift(dc=1))
    with jax.named_scope("update"):
        modified, selected = first_update(update_list, factor_one, panel_two, whole)
    with jax.named_scope("swap"):
        *halves, modified = lax.optimization_barrier((*halves, modified))
        halves = jnp.concatenate(halves)
        swapped_halves = send(halves, shift(dc=1))
        modified = second_update(modified, selected, (swapped, halves, swapped_halves))
    with jax.named_scope("factor_two"):
        factor_two = final(modified, full_two)
    return factor_one, factor_two


def solution(mesh):
    return jax.shard_map(
        body,
        mesh=mesh,
        in_specs=(
            P(("row", "col"), None),
            P(("row", "col"), None),
            P(None, "col"),
            P(None, "col"),
            P(("row", "col"), None),
        ),
        out_specs=(P(("row", "col"), None), P(("row", "col"), None)),
        check_vma=False,
    )
```

```python
import jax
import jax.numpy as jnp
from jax import lax
from jax.experimental import pallas as pl
from jax.experimental.pallas import tpu as pltpu
from jax.sharding import PartitionSpec as P

SN = 2048
B = 256
ROWS = 512
KEEP = 1152
PIECE = 32
BF = jnp.bfloat16
F32 = jnp.float32
AXES = ("row", "col")
SIZES = (4, 4, 8, 2)
ANY = pl.BlockSpec(memory_space=pl.ANY)
SMEM = pl.BlockSpec(memory_space=pltpu.SMEM)
VMEM = pl.BlockSpec(memory_space=pltpu.VMEM)


def device(x, y, z, c):
    return (x * 4 + y) * 16 + z * 2 + c


def shift(dx=0, dy=0, dz=0, dc=0):
    pairs = []
    for x in range(4):
        for y in range(4):
            for z in range(8):
                for c in range(2):
                    to = device((x + dx) % 4, (y + dy) % 4, (z + dz) % 8, (c + dc) % 2)
                    pairs.append((device(x, y, z, c), to))
    return pairs


def along_z(moves):
    return [
        (r * 16 + a * 2 + c, r * 16 + b * 2 + c) for r in range(16) for a, b in moves for c in range(2)
    ]


def send(value, pairs):
    return lax.ppermute(value, AXES, pairs)


ORDER = (
    ((0, 0), (0, 1), (1, 1), (0, 2)),
    ((1, 0), (1, 2), (2, 0), (1, 3)),
    ((0, 3), (2, 2), (2, 3), (3, 3)),
    ((3, 0), (3, 2), (2, 1), (3, 1)),
)
NEAR = ((0, 1), (1, 0), (0, 3), (3, 0))


def in_plane(moves):
    return [(device(*a, 0, d), device(*b, 0, d)) for a, b in moves for d in range(4)]


MIRROR = [(r * 16 + c, r * 16 + 15 - c) for r in range(16) for c in range(9, 16)]


def tail_of(inverse):
    return inverse[KEEP:].reshape(7, 128, 128)[::-1].reshape(7 * 128, 128)


def packed(inverse, tail):
    return inverse[:KEEP] + jnp.concatenate([jnp.zeros((256, 128), BF), tail], axis=0)


def unpack_square(g, w, sems):
    for c in range(16):
        rows = ((c | 1) + 1) * 128
        pltpu.make_async_copy(
            g.at[pl.ds(c * SN, rows)], w.at[pl.ds(0, rows), pl.ds(c * 128, 128)], sems.at[c // 2]
        ).start()


def unpack(g, w, sems):
    for c in range(16):
        sem = sems.at[c // 2]
        count = (c | 1) + 1
        lead = min(count, 9)
        columns = pl.ds(c * 128, 128)
        pltpu.make_async_copy(
            g.at[pl.ds(c * KEEP, lead * 128)], w.at[pl.ds(0, lead * 128), columns], sem
        ).start()
        for h in range(9, count):
            pltpu.make_async_copy(
                g.at[pl.ds((15 - c) * KEEP + (17 - h) * 128, 128)],
                w.at[pl.ds(h * 128, 128), columns],
                sem,
            ).start()


def unpacked(w, sems, j):
    part = w.at[pl.ds(0, (j + 1) * 256), pl.ds(j * 256, 256)]
    pltpu.make_async_copy(part, part, sems.at[j]).wait()


def position():
    row, col = lax.axis_index("row"), lax.axis_index("col")
    return row // 4, row % 4, col // 2, col % 2


def pick_kernel(entries, panel, *refs):
    outs = refs[:4]
    rows, in_sems, sems = refs[4:]
    half_b = position()[2] > 0
    copies = []
    for j in range(2):
        start = pl.multiple_of(jnp.maximum(entries[0, j], 0) * B, B)
        copy = pltpu.make_async_copy(
            panel.at[pl.ds(start, B)], rows.at[pl.ds(j * B, B)], in_sems.at[j]
        )
        copy.start()
        copies.append(copy)
    for copy in copies:
        copy.wait()
    copies = []
    for k, group in enumerate(ORDER):
        for i, (x, y) in enumerate(group):
            start = jnp.where(half_b, 4 * x + y, 4 * y + x) * PIECE
            copy = pltpu.make_async_copy(
                rows.at[pl.ds(pl.multiple_of(start, PIECE), PIECE)],
                outs[k].at[pl.ds(i * PIECE, PIECE)],
                sems.at[k, i],
            )
            copy.start()
            copies.append(copy)
    for copy in copies:
        copy.wait()


def pick(entries, panel):
    return pl.pallas_call(
        pick_kernel,
        out_shape=[jax.ShapeDtypeStruct((4 * PIECE, SN), BF)] * 4,
        in_specs=[SMEM, ANY],
        out_specs=[ANY] * 4,
        scratch_shapes=[
            pltpu.VMEM((ROWS, SN), BF),
            pltpu.SemaphoreType.DMA((2,)),
            pltpu.SemaphoreType.DMA((4, 4)),
        ],
        compiler_params=pltpu.CompilerParams(vmem_limit_bytes=40 << 20),
        cost_estimate=pl.CostEstimate(flops=0, bytes_accessed=4 << 20, transcendentals=0),
    )(entries, panel)


def halves_kernel(*refs):
    ins, outs = refs[:4], refs[4:8]
    whole, rows, in_sems, sems, whole_sem = refs[8:]
    copies = []
    for k in range(4):
        copy = pltpu.make_async_copy(ins[k], rows.at[pl.ds(k * 128, 128)], in_sems.at[k])
        copy.start()
        copies.append(copy)
    for k in range(4):
        copies[k].wait()
        copy = pltpu.make_async_copy(
            rows.at[pl.ds(k * 128 + k % 2 * 64, 64)], outs[k], sems.at[k]
        )
        copy.start()
        copies.append(copy)
    copy = pltpu.make_async_copy(rows, whole, whole_sem)
    copy.start()
    copies.append(copy)
    for copy in copies[4:]:
        copy.wait()


def halves_of(arrays):
    return pl.pallas_call(
        halves_kernel,
        out_shape=[jax.ShapeDtypeStruct((64, SN), BF)] * 4 + [jax.ShapeDtypeStruct((512, SN), BF)],
        in_specs=[ANY] * 4,
        out_specs=[ANY] * 5,
        scratch_shapes=[
            pltpu.VMEM((512, SN), BF),
            pltpu.SemaphoreType.DMA((4,)),
            pltpu.SemaphoreType.DMA((4,)),
            pltpu.SemaphoreType.DMA,
        ],
        compiler_params=pltpu.CompilerParams(vmem_limit_bytes=8 << 20),
        cost_estimate=pl.CostEstimate(flops=0, bytes_accessed=5 << 20, transcendentals=0),
    )(*arrays)


def square_kernel(g, w, sems):
    unpack_square(g, w, sems)
    for j in range(8):
        unpacked(w, sems, j)


def square(gathered):
    return pl.pallas_call(
        square_kernel,
        out_shape=jax.ShapeDtypeStruct((SN, SN), BF),
        in_specs=[ANY],
        out_specs=VMEM,
        scratch_shapes=[pltpu.SemaphoreType.DMA((8,))],
        compiler_params=pltpu.CompilerParams(vmem_limit_bytes=40 << 20),
        cost_estimate=pl.CostEstimate(flops=0, bytes_accessed=13 << 20, transcendentals=0),
    )(gathered)


def panel_rows_kernel(*refs):
    ins, w, la, lb, lab, x, sems = refs[:8], *refs[8:]
    place = position()
    copies = []
    for k, ref in enumerate(ins):
        at = (k // 4) * 128 + ((place[k // 4] + 4 - k % 4) % 4) * PIECE
        copy = pltpu.make_async_copy(ref, x.at[pl.ds(pl.multiple_of(at, PIECE), PIECE)], sems.at[k])
        copy.start()
        copies.append(copy)
    for copy in copies:
        copy.wait()
    for j in range(8):
        columns = pl.ds(j * 256, 256)
        depth = (j + 1) * 256
        result = jnp.dot(
            x[:, pl.ds(0, depth)], w[pl.ds(0, depth), columns], preferred_element_type=F32
        ).astype(BF)
        lab[:, columns] = result
        la[:, columns] = result[:128]
        lb[:, columns] = result[128:]


def panel_rows(arrays, w):
    return pl.pallas_call(
        panel_rows_kernel,
        out_shape=[jax.ShapeDtypeStruct((n, SN), BF) for n in (128, 128, 256)],
        in_specs=[ANY] * 8 + [VMEM],
        out_specs=[VMEM] * 3,
        scratch_shapes=[pltpu.VMEM((256, SN), BF), pltpu.SemaphoreType.DMA((8,))],
        compiler_params=pltpu.CompilerParams(vmem_limit_bytes=16 << 20),
        cost_estimate=pl.CostEstimate(
            flops=256 * SN * SN, bytes_accessed=14 << 20, transcendentals=0
        ),
    )(*arrays, w)


def product_kernel(x, w, out, o, sems):
    copies = []
    for j in range(8):
        columns = pl.ds(j * 256, 256)
        depth = (j + 1) * 256
        o[:, columns] = jnp.dot(
            x[:, pl.ds(0, depth)], w[pl.ds(0, depth), columns], preferred_element_type=F32
        ).astype(BF)
        copy = pltpu.make_async_copy(o.at[:, columns], out.at[:, columns], sems.at[j])
        copy.start()
        copies.append(copy)
    for copy in copies:
        copy.wait()


def product(x, w):
    return pl.pallas_call(
        product_kernel,
        out_shape=jax.ShapeDtypeStruct((ROWS, SN), BF),
        in_specs=[VMEM, VMEM],
        out_specs=ANY,
        scratch_shapes=[pltpu.VMEM((ROWS, SN), BF), pltpu.SemaphoreType.DMA((8,))],
        compiler_params=pltpu.CompilerParams(vmem_limit_bytes=16 << 20),
        cost_estimate=pl.CostEstimate(
            flops=ROWS * SN * SN, bytes_accessed=12 << 20, transcendentals=0
        ),
    )(x, w)


def column_of(place, own, half, back):
    core = place[3] if own else 1 - place[3]
    coordinate = place[0] if half else place[1]
    return pl.multiple_of(((2 * half + core) * 4 + (coordinate + 4 - back) % 4) * 128, 128)


FIRST = (
    ((1, 0, 0), (1, 1, 0)),
    ((0, 0, 0), (0, 1, 0)),
    ((1, 0, 1), (1, 0, 3), (1, 1, 1), (1, 1, 3)),
)
SECOND = (
    ((0, 0, 1), (0, 0, 3), (0, 1, 1), (0, 1, 3)),
    ((1, 0, 2), (1, 1, 2)),
    ((0, 0, 2), (0, 1, 2)),
)


def subtract(parts, s, sources, old, new):
    place = position()
    for source, blocks in zip(sources, parts):
        for k in range(0, len(blocks), 2):
            update = lax.dot_general(
                s[...],
                source[pl.ds(k * 128, 256), :],
                (((1,), (1,)), ((), ())),
                preferred_element_type=F32,
            )
            for i in range(2):
                own = pl.ds(column_of(place, *blocks[k + i]), 128)
                part = update[:, i * 128 : (i + 1) * 128]
                new[:, own] = (old[:, own].astype(F32) - part).astype(BF)


def first_kernel(entries, f1, panel, one, two, three, m, s, s_sems, m_sem):
    copies = []
    for j in range(2):
        start = pl.multiple_of(jnp.maximum(entries[0, j], 0) * B, B)
        copy = pltpu.make_async_copy(f1.at[pl.ds(start, B)], s.at[pl.ds(j * B, B)], s_sems.at[j])
        copy.start()
        copies.append(copy)
    copies.append(pltpu.make_async_copy(panel, m, m_sem))
    copies[-1].start()
    for copy in copies:
        copy.wait()
    for j in range(2):

        @pl.when(entries[0, j] < 0)
        def _(j=j):
            s[pl.ds(j * B, B), :] = jnp.zeros((B, SN), BF)

    subtract(FIRST, s, (one, two, three), m, m)


def first_update(entries, factor_one, panel, sources):
    return pl.pallas_call(
        first_kernel,
        out_shape=[jax.ShapeDtypeStruct((ROWS, SN), BF)] * 2,
        in_specs=[SMEM, ANY, ANY] + [VMEM] * 3,
        out_specs=[VMEM] * 2,
        scratch_shapes=[pltpu.SemaphoreType.DMA((2,)), pltpu.SemaphoreType.DMA],
        compiler_params=pltpu.CompilerParams(vmem_limit_bytes=16 << 20),
        cost_estimate=pl.CostEstimate(
            flops=ROWS * SN * SN, bytes_accessed=12 << 20, transcendentals=0
        ),
    )(entries, factor_one, panel, *sources)


def second_kernel(old, s, one, two, three, new):
    place = position()
    subtract(SECOND, s, (one, two, three), old, new)
    for blocks in FIRST:
        for block in blocks:
            own = pl.ds(column_of(place, *block), 128)
            new[:, own] = old[:, own]


def second_update(modified, selected, sources):
    return pl.pallas_call(
        second_kernel,
        out_shape=jax.ShapeDtypeStruct((ROWS, SN), BF),
        in_specs=[VMEM] * 5,
        out_specs=VMEM,
        compiler_params=pltpu.CompilerParams(vmem_limit_bytes=16 << 20),
        cost_estimate=pl.CostEstimate(
            flops=ROWS * SN * SN, bytes_accessed=12 << 20, transcendentals=0
        ),
    )(modified, selected, *sources)


def final_kernel(m, g, out, w, o, w_sems, o_sems):
    unpack(g, w, w_sems)
    for j in range(8):
        unpacked(w, w_sems, j)
    product_kernel(m, w, out, o, o_sems)


def final(modified, gathered):
    return pl.pallas_call(
        final_kernel,
        out_shape=jax.ShapeDtypeStruct((ROWS, SN), BF),
        in_specs=[VMEM, ANY],
        out_specs=ANY,
        scratch_shapes=[
            pltpu.VMEM((SN, SN), BF),
            pltpu.VMEM((ROWS, SN), BF),
            pltpu.SemaphoreType.DMA((8,)),
            pltpu.SemaphoreType.DMA((8,)),
        ],
        compiler_params=pltpu.CompilerParams(vmem_limit_bytes=50 << 20),
        cost_estimate=pl.CostEstimate(
            flops=ROWS * SN * SN, bytes_accessed=9 << 20, transcendentals=0
        ),
    )(modified, gathered)


def body(panel_one, panel_two, inverse_one, inverse_two, update_list):
    row, col = lax.axis_index("row"), lax.axis_index("col")
    z = col // 2

    with jax.named_scope("inverse_one"):
        full_one = lax.all_gather(inverse_one, "col", axis=0, tiled=True)

    with jax.named_scope("scatter_rows"):
        groups = pick(update_list, panel_one)
        parts = [send(groups[k], in_plane([((0, 0), NEAR[k])])) for k in range(4)]

    with jax.named_scope("forward_rows"):
        near = parts[0] + parts[1] + parts[2] + parts[3]
        kept = jnp.where(row == NEAR[0][1], near[32:64], near[:32])
        piece = jnp.where(row == 0, groups[0][:32], kept)
        for i in range(1, 4):
            moves = [(NEAR[k], ORDER[k][i]) for k in range(4) if NEAR[k] != ORDER[k][i]]
            piece = piece + send(near[i * 32 : (i + 1) * 32], in_plane(moves))

    with jax.named_scope("along_z"):
        piece = jnp.where(z < 2, piece, 0)
        piece = (
            piece
            + send(piece, along_z([(0, 2), (1, 3)]))
            + send(piece, along_z([(0, 6), (1, 7)]))
            + send(piece, along_z([(0, 4), (1, 5)]))
        )
        other = send(piece, along_z([(k, k ^ 1) for k in range(8)]))
        even = z % 2 == 0
        a, b = jnp.where(even, piece, other), jnp.where(even, other, piece)

    with jax.named_scope("inverse_two"):
        inverse_two, a, b = lax.optimization_barrier((inverse_two, a, b))
        tail = send(tail_of(inverse_two), MIRROR)

    with jax.named_scope("first_gather"):
        a_all = [a, send(a, shift(dx=1)), send(a, shift(dx=2)), send(a, shift(dx=-1))]
        b_all = [b, send(b, shift(dy=1)), send(b, shift(dy=2)), send(b, shift(dy=-1))]

    with jax.named_scope("inverse_two"):
        tail, *_ = lax.optimization_barrier((tail, *a_all, *b_all))
        full_two = lax.all_gather(packed(inverse_two, tail), "col", axis=0, tiled=True)

    with jax.named_scope("panel_rows"):
        whole_one = square(full_one)
        la, lb, lab = panel_rows(a_all + b_all, whole_one)

    with jax.named_scope("factor_one"):
        rows, _ = lax.optimization_barrier((panel_one, lab))
        factor_one = product(rows, whole_one)

    with jax.named_scope("second_gather"):
        a1, a3 = send(la, shift(dy=1)), send(la, shift(dy=-1))
        b1, b3 = send(lb, shift(dx=1)), send(lb, shift(dx=-1))
        theirs = send(lab, shift(dc=1))
        a1, a3, b1, b3, factor_one = lax.optimization_barrier((a1, a3, b1, b3, factor_one))
        *halves, whole = halves_of((a1, a3, b1, b3))
        moves = (shift(dy=1), shift(dy=-1), shift(dx=1), shift(dx=-1))
        halves = [send(v, m) for v, m in zip(halves, moves)]
        swapped = send(whole, shift(dc=1))
    with jax.named_scope("update"):
        modified, selected = first_update(update_list, factor_one, panel_two, (lab, theirs, whole))
    with jax.named_scope("swap"):
        *halves, modified = lax.optimization_barrier((*halves, modified))
        halves = jnp.concatenate(halves)
        swapped_halves = send(halves, shift(dc=1))
        modified = second_update(modified, selected, (swapped, halves, swapped_halves))
    with jax.named_scope("factor_two"):
        factor_two = final(modified, full_two)
    return factor_one, factor_two


def solution(mesh):
    return jax.shard_map(
        body,
        mesh=mesh,
        in_specs=(
            P(("row", "col"), None),
            P(("row", "col"), None),
            P(None, "col"),
            P(None, "col"),
            P(("row", "col"), None),
        ),
        out_specs=(P(("row", "col"), None), P(("row", "col"), None)),
        check_vma=False,
    )
```

```python
import jax
import jax.numpy as jnp
from jax import lax
from jax.experimental import pallas as pl
from jax.experimental.pallas import tpu as pltpu
from jax.sharding import PartitionSpec as P

SN = 2048
B = 256
ROWS = 512
KEEP = 1152
PIECE = 32
BF = jnp.bfloat16
F32 = jnp.float32
AXES = ("row", "col")
SIZES = (4, 4, 8, 2)
ANY = pl.BlockSpec(memory_space=pl.ANY)
SMEM = pl.BlockSpec(memory_space=pltpu.SMEM)
VMEM = pl.BlockSpec(memory_space=pltpu.VMEM)


def device(x, y, z, c):
    return (x * 4 + y) * 16 + z * 2 + c


def shift(dx=0, dy=0, dz=0, dc=0):
    pairs = []
    for x in range(4):
        for y in range(4):
            for z in range(8):
                for c in range(2):
                    to = device((x + dx) % 4, (y + dy) % 4, (z + dz) % 8, (c + dc) % 2)
                    pairs.append((device(x, y, z, c), to))
    return pairs


def along_z(moves):
    return [
        (r * 16 + a * 2 + c, r * 16 + b * 2 + c) for r in range(16) for a, b in moves for c in range(2)
    ]


def send(value, pairs):
    return lax.ppermute(value, AXES, pairs)


ORDER = (
    ((0, 0), (0, 1), (1, 1), (0, 2)),
    ((1, 0), (1, 2), (2, 0), (1, 3)),
    ((0, 3), (2, 2), (2, 3), (3, 3)),
    ((3, 0), (3, 2), (2, 1), (3, 1)),
)
NEAR = ((0, 1), (1, 0), (0, 3), (3, 0))


def in_plane(moves):
    return [(device(*a, 0, d), device(*b, 0, d)) for a, b in moves for d in range(4)]


MIRROR = [(r * 16 + c, r * 16 + 15 - c) for r in range(16) for c in range(9, 16)]


def tail_of(inverse):
    return inverse[KEEP:].reshape(7, 128, 128)[::-1].reshape(7 * 128, 128)


def packed(inverse, tail):
    return inverse[:KEEP] + jnp.concatenate([jnp.zeros((256, 128), BF), tail], axis=0)


def unpack_square(g, w, sems):
    for c in range(16):
        rows = ((c | 1) + 1) * 128
        pltpu.make_async_copy(
            g.at[pl.ds(c * SN, rows)], w.at[pl.ds(0, rows), pl.ds(c * 128, 128)], sems.at[c // 2]
        ).start()


def unpack(g, w, sems):
    for c in range(16):
        sem = sems.at[c // 2]
        count = (c | 1) + 1
        lead = min(count, 9)
        columns = pl.ds(c * 128, 128)
        pltpu.make_async_copy(
            g.at[pl.ds(c * KEEP, lead * 128)], w.at[pl.ds(0, lead * 128), columns], sem
        ).start()
        for h in range(9, count):
            pltpu.make_async_copy(
                g.at[pl.ds((15 - c) * KEEP + (17 - h) * 128, 128)],
                w.at[pl.ds(h * 128, 128), columns],
                sem,
            ).start()


def unpacked(w, sems, j):
    part = w.at[pl.ds(0, (j + 1) * 256), pl.ds(j * 256, 256)]
    pltpu.make_async_copy(part, part, sems.at[j]).wait()


def position():
    row, col = lax.axis_index("row"), lax.axis_index("col")
    return row // 4, row % 4, col // 2, col % 2


def pick_kernel(entries, panel, *refs):
    outs = refs[:4]
    rows, in_sems, sems = refs[4:]
    half_b = position()[2] > 0
    copies = []
    for j in range(2):
        start = pl.multiple_of(jnp.maximum(entries[0, j], 0) * B, B)
        copy = pltpu.make_async_copy(
            panel.at[pl.ds(start, B)], rows.at[pl.ds(j * B, B)], in_sems.at[j]
        )
        copy.start()
        copies.append(copy)
    for copy in copies:
        copy.wait()
    copies = []
    for k, group in enumerate(ORDER):
        for i, (x, y) in enumerate(group):
            start = jnp.where(half_b, 4 * x + y, 4 * y + x) * PIECE
            copy = pltpu.make_async_copy(
                rows.at[pl.ds(pl.multiple_of(start, PIECE), PIECE)],
                outs[k].at[pl.ds(i * PIECE, PIECE)],
                sems.at[k, i],
            )
            copy.start()
            copies.append(copy)
    for copy in copies:
        copy.wait()


def pick(entries, panel):
    return pl.pallas_call(
        pick_kernel,
        out_shape=[jax.ShapeDtypeStruct((4 * PIECE, SN), BF)] * 4,
        in_specs=[SMEM, ANY],
        out_specs=[ANY] * 4,
        scratch_shapes=[
            pltpu.VMEM((ROWS, SN), BF),
            pltpu.SemaphoreType.DMA((2,)),
            pltpu.SemaphoreType.DMA((4, 4)),
        ],
        compiler_params=pltpu.CompilerParams(vmem_limit_bytes=40 << 20),
        cost_estimate=pl.CostEstimate(flops=0, bytes_accessed=4 << 20, transcendentals=0),
    )(entries, panel)


def halves_kernel(*refs):
    ins, outs = refs[:5], refs[5:9]
    whole, rows, in_sems, sems, whole_sem = refs[9:]
    copies = []
    for k in range(5):
        copy = pltpu.make_async_copy(
            ins[k], rows.at[pl.ds(k * 128, 256 if k == 4 else 128)], in_sems.at[k]
        )
        copy.start()
        copies.append(copy)
    for k in range(4):
        copies[k].wait()
        copy = pltpu.make_async_copy(
            rows.at[pl.ds(k * 128 + k % 2 * 64, 64)], outs[k], sems.at[k]
        )
        copy.start()
        copies.append(copy)
    copies[4].wait()
    copy = pltpu.make_async_copy(rows, whole, whole_sem)
    copy.start()
    copies.append(copy)
    for copy in copies[5:]:
        copy.wait()


def halves_of(arrays):
    return pl.pallas_call(
        halves_kernel,
        out_shape=[jax.ShapeDtypeStruct((64, SN), BF)] * 4 + [jax.ShapeDtypeStruct((768, SN), BF)],
        in_specs=[ANY] * 5,
        out_specs=[ANY] * 5,
        scratch_shapes=[
            pltpu.VMEM((768, SN), BF),
            pltpu.SemaphoreType.DMA((5,)),
            pltpu.SemaphoreType.DMA((4,)),
            pltpu.SemaphoreType.DMA,
        ],
        compiler_params=pltpu.CompilerParams(vmem_limit_bytes=8 << 20),
        cost_estimate=pl.CostEstimate(flops=0, bytes_accessed=5 << 20, transcendentals=0),
    )(*arrays)


def square_kernel(g, w, sems):
    unpack_square(g, w, sems)
    for j in range(8):
        unpacked(w, sems, j)


def square(gathered):
    return pl.pallas_call(
        square_kernel,
        out_shape=jax.ShapeDtypeStruct((SN, SN), BF),
        in_specs=[ANY],
        out_specs=VMEM,
        scratch_shapes=[pltpu.SemaphoreType.DMA((8,))],
        compiler_params=pltpu.CompilerParams(vmem_limit_bytes=40 << 20),
        cost_estimate=pl.CostEstimate(flops=0, bytes_accessed=13 << 20, transcendentals=0),
    )(gathered)


def panel_rows_kernel(*refs):
    ins, w, la, lb, lab, x, sems = refs[:8], *refs[8:]
    place = position()
    copies = []
    for k, ref in enumerate(ins):
        at = (k // 4) * 128 + ((place[k // 4] + 4 - k % 4) % 4) * PIECE
        copy = pltpu.make_async_copy(ref, x.at[pl.ds(pl.multiple_of(at, PIECE), PIECE)], sems.at[k])
        copy.start()
        copies.append(copy)
    for copy in copies:
        copy.wait()
    for j in range(8):
        columns = pl.ds(j * 256, 256)
        depth = (j + 1) * 256
        result = jnp.dot(
            x[:, pl.ds(0, depth)], w[pl.ds(0, depth), columns], preferred_element_type=F32
        ).astype(BF)
        lab[:, columns] = result
        la[:, columns] = result[:128]
        lb[:, columns] = result[128:]


def panel_rows(arrays, w):
    return pl.pallas_call(
        panel_rows_kernel,
        out_shape=[jax.ShapeDtypeStruct((n, SN), BF) for n in (128, 128, 256)],
        in_specs=[ANY] * 8 + [VMEM],
        out_specs=[VMEM] * 3,
        scratch_shapes=[pltpu.VMEM((256, SN), BF), pltpu.SemaphoreType.DMA((8,))],
        compiler_params=pltpu.CompilerParams(vmem_limit_bytes=16 << 20),
        cost_estimate=pl.CostEstimate(
            flops=256 * SN * SN, bytes_accessed=14 << 20, transcendentals=0
        ),
    )(*arrays, w)


def product_kernel(x, w, out, o, sems):
    copies = []
    for j in range(8):
        columns = pl.ds(j * 256, 256)
        depth = (j + 1) * 256
        o[:, columns] = jnp.dot(
            x[:, pl.ds(0, depth)], w[pl.ds(0, depth), columns], preferred_element_type=F32
        ).astype(BF)
        copy = pltpu.make_async_copy(o.at[:, columns], out.at[:, columns], sems.at[j])
        copy.start()
        copies.append(copy)
    for copy in copies:
        copy.wait()


def product(x, w):
    return pl.pallas_call(
        product_kernel,
        out_shape=jax.ShapeDtypeStruct((ROWS, SN), BF),
        in_specs=[VMEM, VMEM],
        out_specs=ANY,
        scratch_shapes=[pltpu.VMEM((ROWS, SN), BF), pltpu.SemaphoreType.DMA((8,))],
        compiler_params=pltpu.CompilerParams(vmem_limit_bytes=16 << 20),
        cost_estimate=pl.CostEstimate(
            flops=ROWS * SN * SN, bytes_accessed=12 << 20, transcendentals=0
        ),
    )(x, w)


def column_of(place, own, half, back):
    core = place[3] if own else 1 - place[3]
    coordinate = place[0] if half else place[1]
    return pl.multiple_of(((2 * half + core) * 4 + (coordinate + 4 - back) % 4) * 128, 128)


FIRST = (((1, 0, 1), (1, 0, 3), (1, 1, 1), (1, 1, 3), (1, 0, 0), (1, 1, 0)),)
SECOND = (
    ((0, 0, 1), (0, 0, 3), (0, 1, 1), (0, 1, 3), (0, 0, 0), (0, 1, 0)),
    ((1, 0, 2), (1, 1, 2)),
    ((0, 0, 2), (0, 1, 2)),
)


def subtract(parts, s, sources, old, new):
    place = position()
    for source, blocks in zip(sources, parts):
        for k in range(0, len(blocks), 2):
            update = lax.dot_general(
                s[...],
                source[pl.ds(k * 128, 256), :],
                (((1,), (1,)), ((), ())),
                preferred_element_type=F32,
            )
            for i in range(2):
                own = pl.ds(column_of(place, *blocks[k + i]), 128)
                part = update[:, i * 128 : (i + 1) * 128]
                new[:, own] = (old[:, own].astype(F32) - part).astype(BF)


def first_kernel(entries, f1, panel, own, m, s, s_sems, m_sem):
    copies = []
    for j in range(2):
        start = pl.multiple_of(jnp.maximum(entries[0, j], 0) * B, B)
        copy = pltpu.make_async_copy(f1.at[pl.ds(start, B)], s.at[pl.ds(j * B, B)], s_sems.at[j])
        copy.start()
        copies.append(copy)
    copies.append(pltpu.make_async_copy(panel, m, m_sem))
    copies[-1].start()
    for copy in copies:
        copy.wait()
    for j in range(2):

        @pl.when(entries[0, j] < 0)
        def _(j=j):
            s[pl.ds(j * B, B), :] = jnp.zeros((B, SN), BF)

    subtract(FIRST, s, (own,), m, m)


def first_update(entries, factor_one, panel, own):
    return pl.pallas_call(
        first_kernel,
        out_shape=[jax.ShapeDtypeStruct((ROWS, SN), BF)] * 2,
        in_specs=[SMEM, ANY, ANY, VMEM],
        out_specs=[VMEM] * 2,
        scratch_shapes=[pltpu.SemaphoreType.DMA((2,)), pltpu.SemaphoreType.DMA],
        compiler_params=pltpu.CompilerParams(vmem_limit_bytes=16 << 20),
        cost_estimate=pl.CostEstimate(
            flops=ROWS * SN * SN, bytes_accessed=12 << 20, transcendentals=0
        ),
    )(entries, factor_one, panel, own)


def second_kernel(old, s, one, two, three, new):
    place = position()
    subtract(SECOND, s, (one, two, three), old, new)
    for blocks in FIRST:
        for block in blocks:
            own = pl.ds(column_of(place, *block), 128)
            new[:, own] = old[:, own]


def second_update(modified, selected, sources):
    return pl.pallas_call(
        second_kernel,
        out_shape=jax.ShapeDtypeStruct((ROWS, SN), BF),
        in_specs=[VMEM] * 5,
        out_specs=VMEM,
        compiler_params=pltpu.CompilerParams(vmem_limit_bytes=16 << 20),
        cost_estimate=pl.CostEstimate(
            flops=ROWS * SN * SN, bytes_accessed=12 << 20, transcendentals=0
        ),
    )(modified, selected, *sources)


def final_kernel(m, g, out, w, o, w_sems, o_sems):
    unpack(g, w, w_sems)
    for j in range(8):
        unpacked(w, w_sems, j)
    product_kernel(m, w, out, o, o_sems)


def final(modified, gathered):
    return pl.pallas_call(
        final_kernel,
        out_shape=jax.ShapeDtypeStruct((ROWS, SN), BF),
        in_specs=[VMEM, ANY],
        out_specs=ANY,
        scratch_shapes=[
            pltpu.VMEM((SN, SN), BF),
            pltpu.VMEM((ROWS, SN), BF),
            pltpu.SemaphoreType.DMA((8,)),
            pltpu.SemaphoreType.DMA((8,)),
        ],
        compiler_params=pltpu.CompilerParams(vmem_limit_bytes=50 << 20),
        cost_estimate=pl.CostEstimate(
            flops=ROWS * SN * SN, bytes_accessed=9 << 20, transcendentals=0
        ),
    )(modified, gathered)


def body(panel_one, panel_two, inverse_one, inverse_two, update_list):
    row, col = lax.axis_index("row"), lax.axis_index("col")
    z = col // 2

    with jax.named_scope("inverse_one"):
        full_one = lax.all_gather(inverse_one, "col", axis=0, tiled=True)

    with jax.named_scope("scatter_rows"):
        groups = pick(update_list, panel_one)
        parts = [send(groups[k], in_plane([((0, 0), NEAR[k])])) for k in range(4)]

    with jax.named_scope("forward_rows"):
        near = parts[0] + parts[1] + parts[2] + parts[3]
        kept = jnp.where(row == NEAR[0][1], near[32:64], near[:32])
        piece = jnp.where(row == 0, groups[0][:32], kept)
        for i in range(1, 4):
            moves = [(NEAR[k], ORDER[k][i]) for k in range(4) if NEAR[k] != ORDER[k][i]]
            piece = piece + send(near[i * 32 : (i + 1) * 32], in_plane(moves))

    with jax.named_scope("along_z"):
        piece = jnp.where(z < 2, piece, 0)
        piece = (
            piece
            + send(piece, along_z([(0, 2), (1, 3)]))
            + send(piece, along_z([(0, 6), (1, 7)]))
            + send(piece, along_z([(0, 4), (1, 5)]))
        )
        other = send(piece, along_z([(k, k ^ 1) for k in range(8)]))
        even = z % 2 == 0
        a, b = jnp.where(even, piece, other), jnp.where(even, other, piece)

    with jax.named_scope("inverse_two"):
        inverse_two, a, b = lax.optimization_barrier((inverse_two, a, b))
        tail = send(tail_of(inverse_two), MIRROR)

    with jax.named_scope("first_gather"):
        a_all = [a, send(a, shift(dx=1)), send(a, shift(dx=2)), send(a, shift(dx=-1))]
        b_all = [b, send(b, shift(dy=1)), send(b, shift(dy=2)), send(b, shift(dy=-1))]

    with jax.named_scope("inverse_two"):
        tail, *_ = lax.optimization_barrier((tail, *a_all, *b_all))
        full_two = lax.all_gather(packed(inverse_two, tail), "col", axis=0, tiled=True)

    with jax.named_scope("panel_rows"):
        whole_one = square(full_one)
        la, lb, lab = panel_rows(a_all + b_all, whole_one)

    with jax.named_scope("factor_one"):
        rows, _ = lax.optimization_barrier((panel_one, lab))
        factor_one = product(rows, whole_one)

    with jax.named_scope("second_gather"):
        a1, a3 = send(la, shift(dy=1)), send(la, shift(dy=-1))
        b1, b3 = send(lb, shift(dx=1)), send(lb, shift(dx=-1))
        a1, a3, b1, b3, factor_one = lax.optimization_barrier((a1, a3, b1, b3, factor_one))
        *halves, whole = halves_of((a1, a3, b1, b3, lab))
        moves = (shift(dy=1), shift(dy=-1), shift(dx=1), shift(dx=-1))
        halves = [send(v, m) for v, m in zip(halves, moves)]
        swapped = send(whole, shift(dc=1))
    with jax.named_scope("update"):
        modified, selected = first_update(update_list, factor_one, panel_two, whole)
    with jax.named_scope("swap"):
        *halves, modified = lax.optimization_barrier((*halves, modified))
        halves = jnp.concatenate(halves)
        swapped_halves = send(halves, shift(dc=1))
        modified = second_update(modified, selected, (swapped, halves, swapped_halves))
    with jax.named_scope("factor_two"):
        factor_two = final(modified, full_two)
    return factor_one, factor_two


def solution(mesh):
    return jax.shard_map(
        body,
        mesh=mesh,
        in_specs=(
            P(("row", "col"), None),
            P(("row", "col"), None),
            P(None, "col"),
            P(None, "col"),
            P(("row", "col"), None),
        ),
        out_specs=(P(("row", "col"), None), P(("row", "col"), None)),
        check_vma=False,
    )
```
